256 devices in a mesh: chan: 16 (over y, x_hi, core), filt: 16 (over x_lo, z).
Axes of the slice: x: 4 (x_hi: 2, x_lo: 2; x = x_hi * 2 + x_lo), y: 4, z: 8, core: 2. Of those that a mesh axis runs over, the one named last changes fastest.
Arguments:
- activations: bfloat16 [2592, 2048], P(None, ('chan', 'filt')), may hold values from -6 to 6
- act_tangent: bfloat16 [2592, 2048], P(None, ('chan', 'filt')), may hold values from -6 to 6
- kernel: bfloat16 [9, 2048, 2048], P(None, 'chan', 'filt'), may hold values from -0.046875 to 0.046875
- kernel_tangent: bfloat16 [9, 2048, 2048], P(None, 'chan', 'filt'), may hold values from -0.046875 to 0.046875
- slope: bfloat16 [2592, 2048], P('chan', 'filt'), may hold values from 0.19921875 to 1.09375
- curvature: bfloat16 [2592, 2048], P('chan', 'filt'), may hold values from 0.29882812 to 3
Outputs:
- input_cotangent: bfloat16 [2592, 2048], P('filt', 'chan')
- kernel_product: float32 [9, 2048, 2048], P(None, 'chan', 'filt')
The draws below stay inside these ranges and needn't reach their ends.
All inputs are finite; a program needn't handle non-finite values.
Results may differ from the reference program's by a relative error of at most 0.0047.
Values may be sent and summed in bfloat16 or wider, within the bound.
A program may use at most 192 MiB of HBM per device.

```python
import math
import jax
import jax.numpy as jnp

C = 2048
F = 2048
HH = 12
WW = 12
PIXELS = 2592


def level_of(key, extent, pieces, least, largest):
    level = 1.0
    for position, shards_of in pieces:
        heights = jax.random.uniform(jax.random.fold_in(jax.random.fold_in(key, 6), position), (shards_of,), jnp.float32, least / len(pieces), largest / len(pieces))
        level = level * jnp.repeat(jnp.exp(heights), extent[position] // shards_of).reshape((-1,) + (1,) * (len(extent) - 1 - position))
    return level


def scatter_about(key, shape, scale, reach, cuts=(), dtype=jnp.bfloat16):
    values = scale * jax.random.normal(key, shape, jnp.float32)
    if cuts:
        values = values * level_of(key, shape, cuts, -0.22, 0.18)
    return jnp.clip(values, -reach, reach).astype(dtype)


def setup_inputs(seed: int = 0) -> dict:
    seeds = jax.random.split(jax.random.key(seed), 7)
    activations = scatter_about(seeds[0], (PIXELS, C), 1.0, 6.0, ((1, 256),))
    act_tangent = scatter_about(seeds[1], (PIXELS, C), 1.0, 6.0, ((1, 256),))
    kernel = scatter_about(seeds[2], (9, C, F), (9 * C) ** -0.5, 0.046875, ((1, 16), (2, 16)))
    kernel_tangent = scatter_about(seeds[3], (9, C, F), (9 * C) ** -0.5, 0.046875, ((1, 16), (2, 16)))
    slope = jnp.clip(0.19921875 + 0.89453125 * jax.random.uniform(seeds[4], (PIXELS, F), jnp.float32) ** level_of(seeds[4], (PIXELS, F), ((0, 16), (1, 16)), -0.2, 0.2), 0.19921875, 1.09375).astype(jnp.bfloat16)
    curvature = jnp.clip(jnp.exp(math.log(3.0) - 2.306499 * jax.random.uniform(seeds[5], (PIXELS, F), jnp.float32) ** level_of(seeds[5], (PIXELS, F), ((0, 16), (1, 16)), -0.2, 0.2)), 0.29882812, 3.0).astype(jnp.bfloat16)
    return {"activations": activations, "act_tangent": act_tangent, "kernel": kernel, "kernel_tangent": kernel_tangent, "slope": slope, "curvature": curvature}


def windows(flat, flip):
    width = flat.shape[-1]
    image = flat.reshape(-1, HH, WW, width)
    padded = jnp.pad(image, ((0, 0), (1, 1), (1, 1), (0, 0)))
    result = []
    for row_tap in range(3):
        for col_tap in range(3):
            top = 2 - row_tap if flip else row_tap
            left = 2 - col_tap if flip else col_tap
            result.append(padded[:, top:top + HH, left:left + WW, :].reshape(-1, width))
    return result

def reference(activations, act_tangent, kernel, kernel_tangent, slope, curvature):
    acts = windows(activations, False)
    tans = windows(act_tangent, False)
    out_tangent = jnp.zeros((PIXELS, F), jnp.float32)
    for tap in range(9):
        out_tangent = out_tangent + jnp.dot(tans[tap], kernel[tap], preferred_element_type=jnp.float32)
        out_tangent = out_tangent + jnp.dot(acts[tap], kernel_tangent[tap], preferred_element_type=jnp.float32)
    slope_f = slope.astype(jnp.float32)
    weighted = (slope_f * slope_f * curvature.astype(jnp.float32) * out_tangent).astype(jnp.bfloat16)
    backs = windows(weighted, True)
    cotangent = jnp.zeros((PIXELS, C), jnp.float32)
    grads = []
    for tap in range(9):
        cotangent = cotangent + jnp.dot(backs[tap], kernel[tap].T, preferred_element_type=jnp.float32)
        grads.append(jnp.dot(acts[tap].T, weighted, preferred_element_type=jnp.float32))
    kernel_product = jnp.stack(grads) / jnp.sqrt(jnp.float32(PIXELS))
    return (cotangent.astype(jnp.bfloat16), kernel_product)
```

```python
import jax
import jax.numpy as jnp
import numpy as np
from jax import lax
from jax.experimental import pallas as pl
from jax.experimental.pallas import tpu as pltpu
from jax.sharding import PartitionSpec as P

HH = 12
WW = 12
IMAGE = HH * WW
PIXELS = 2592
LANES = 2688
CUT = 1152
SHARE = 162
ROWS = 176
PAD = 16
BLOCK = 384
TAPS = 9
BF = jnp.bfloat16
F32 = jnp.float32


def row_masks():
    r = np.arange(IMAGE + ROWS)
    i, j = (r // WW) % HH, r % WW
    m = np.stack([i >= 1, i <= HH - 2, j >= 1, j <= WW - 2]).astype(np.float32)
    return np.ascontiguousarray(np.broadcast_to(m[:, :, None], (*m.shape, 128)))


def lane_masks():
    p = np.arange(LANES)
    i, j = (p // WW) % HH, p % WW
    m = np.zeros((16, LANES), np.float32)
    for a in range(3):
        for e in range(3):
            si, sj = i + a - 1, j + e - 1
            m[3 * a + e] = (si >= 0) & (si < HH) & (sj >= 0) & (sj < WW) & (p < PIXELS)
    return m


def body(
    acts_ref, tans_ref, w_ref, v_ref, slope_ref, curv_ref, rmask, lmask,
    cot_ref, kp_ref,
    gath, wcat, taps, xts, w32, w16, sib_out, sib_in, red_out, red_in, own,
    wgt, cx_out, cx_in, cz_out, cz_in,
    a_ss, a_rs, p_rs, s_ss, s_rs, b_ss, b_rs, w_ss, w_rs, x_ss, x_rs, d_ss, d_rs,
):
    chan = lax.axis_index("chan")
    filt = lax.axis_index("filt")
    core = lax.rem(chan, 2)
    chip = lax.div(chan, 2)
    half = lax.div(filt, 8)
    z = lax.rem(filt, 8)
    other = 1 - core
    sibling = {"chan": 2 * chip + other, "filt": filt}
    across = {"chan": chan, "filt": (1 - half) * 8 + z}

    def at_z(d):
        return lax.rem(z + d + 8, 8)

    def z_dev(d):
        return {"chan": chan, "filt": half * 8 + at_z(d)}

    def chip_at(d):
        return lax.rem(chip + d + 8, 8)

    def chip_dev(d):
        return {"chan": 2 * chip_at(d) + core, "filt": filt}

    def remote(src, dst, ss, rs, dev):
        return pltpu.make_async_remote_copy(
            src_ref=src, dst_ref=dst, send_sem=ss, recv_sem=rs,
            device_id=dev, device_id_type=pl.DeviceIdType.MESH,
        )

    barrier = pltpu.get_barrier_semaphore()
    peers = [sibling, across]
    peers += [z_dev(d) for d in range(1, 8)] + [chip_dev(d) for d in range(1, 8)]
    for dev in peers:
        pl.semaphore_signal(barrier, inc=1, device_id=dev, device_id_type=pl.DeviceIdType.MESH)

    both = jnp.concatenate([acts_ref[...].astype(F32), tans_ref[...].astype(F32)], axis=0)
    both = jnp.concatenate([both, jnp.zeros((16, LANES - PIXELS), F32)], axis=1)
    gath[filt] = both.astype(BF)
    pl.semaphore_wait(barrier, len(peers))

    mine = half * 8
    theirs = (1 - half) * 8
    sent = []

    def send_full(slot, dev):
        n = len(sent)
        c = remote(gath.at[slot], gath.at[slot], a_ss.at[n], a_rs.at[slot], dev)
        c.start()
        sent.append(c)

    def low(slot):
        return gath.at[slot, :, pl.ds(0, CUT)]

    def high(slot):
        return gath.at[slot, :, pl.ds(CUT, LANES - CUT)]

    def send_low(slot, dev):
        n = len(sent)
        c = remote(low(slot), low(slot), a_ss.at[n], a_rs.at[slot], dev)
        c.start()
        sent.append(c)

    def send_high(slot, dev):
        n = len(sent)
        c = remote(high(slot), high(slot), a_ss.at[n], p_rs.at[slot], dev)
        c.start()
        sent.append(c)

    def got_full(slot):
        remote(gath.at[slot], gath.at[slot], a_ss.at[0], a_rs.at[slot], across).wait_recv()

    def got_low(slot):
        remote(low(slot), low(slot), a_ss.at[0], a_rs.at[slot], across).wait_recv()

    def got_high(slot):
        remote(high(slot), high(slot), a_ss.at[0], p_rs.at[slot], across).wait_recv()

    right, left = z_dev(1), z_dev(-1)
    send_full(filt, right)
    send_full(filt, left)
    send_full(filt, across)

    for k in range(TAPS):
        vk = v_ref[k].astype(F32).reshape(16, 1, 8, 128)
        wk = w_ref[k].astype(F32).reshape(16, 1, 8, 128)
        wcat[:, 128 * k:128 * k + 128] = (
            jnp.concatenate([vk, wk], axis=1).reshape(256, 128).astype(BF)
        )
        taps[k, 0:PAD, :] = jnp.zeros((PAD, 128), F32)

    for h in range(1, 6):
        if h <= 4:
            slot = mine + at_z(-h)
            got_full(slot)
            if h < 4:
                send_full(slot, right)
            send_high(slot, across)
        if h <= 3:
            slot = mine + at_z(h)
            got_full(slot)
            if h < 3:
                send_full(slot, left)
            send_high(slot, across)
        if h == 1:
            slot = theirs + z
            got_full(slot)
            send_low(slot, right)
            send_low(slot, left)
        else:
            slot = theirs + at_z(-(h - 1))
            got_low(slot)
            if h - 1 < 4:
                send_low(slot, right)
            if h - 1 <= 3:
                slot = theirs + at_z(h - 1)
                got_low(slot)
                if h - 1 < 3:
                    send_low(slot, left)
    for d in range(1, 8):
        got_high(theirs + at_z(d))

    def forward(t, _):
        lanes = pl.ds(pl.multiple_of(t * BLOCK, 128), BLOCK)
        rows = pl.ds(pl.multiple_of(PAD + t * BLOCK, 16), BLOCK)
        x = gath[:, :, lanes].reshape(256, BLOCK).T
        for k in range(0, TAPS, 2):
            width = min(2, TAPS - k)
            res = jnp.dot(x, wcat[:, 128 * k:128 * (k + width)], preferred_element_type=F32)
            for q in range(width):
                taps[k + q, rows, :] = res[:, 128 * q:128 * q + 128]
        return 0

    lax.fori_loop(0, LANES // BLOCK, forward, 0)

    def combined(c, flip, put):
        start = c * SHARE
        within = lax.rem(start, IMAGE)
        step = ROWS // 2
        for s in range(0, ROWS, step):
            m = [rmask[n, pl.ds(within + s, step), :] for n in range(4)]
            acc = None
            for a in range(3):
                part = None
                for e in range(3):
                    k = 3 * a + e
                    off = WW * (a - 1) + e - 1
                    val = taps[8 - k if flip else k, pl.ds(PAD + start + s + off, step), :]
                    if e == 0:
                        val = val * m[2]
                    if e == 2:
                        val = val * m[3]
                    part = val if part is None else part + val
                if a == 0:
                    part = part * m[0]
                if a == 2:
                    part = part * m[1]
                acc = part if acc is None else acc + part
            put(s, step, acc)

    def sib_copy(d):
        return remote(sib_out.at[d], sib_in.at[d], s_ss.at[d], s_rs.at[d], sibling)

    def to_sibling(j, _):
        d = chip_at(j + 1)

        def put(s, n, acc):
            sib_out[d, s:s + n, :] = acc

        combined(2 * d + other, False, put)
        sib_copy(d).start()
        return 0

    lax.fori_loop(0, 8, to_sibling, 0)

    def red_copy(j):
        d = chip_at(j)
        return remote(red_out.at[j], red_in.at[j], b_ss.at[j], b_rs.at[j], chip_dev(j))

    def to_chip(j, _):
        d = chip_at(j)
        sib_copy(d).wait_recv()

        def put(s, n, acc):
            red_out[j, s:s + n, :] = (acc + sib_in[d, s:s + n, :]).astype(BF)

        combined(2 * d + core, False, put)
        red_copy(j).start()
        return 0

    lax.fori_loop(1, 8, to_chip, 0)
    sib_copy(chip).wait_recv()

    def put_own(s, n, acc):
        own[s:s + n, :] = acc + sib_in[chip, s:s + n, :]

    combined(2 * chip + core, False, put_own)

    def shift(t, _):
        g = gath[pl.ds(2 * t, 2)].astype(F32)
        x = g[:, 0:8, :].reshape(16, LANES)
        rows = pl.ds(pl.multiple_of(16 * t, 16), 16)
        for e in range(3):
            xe = x if e == 1 else pltpu.roll(x, (1 - e) % LANES, 1)
            for a in range(3):
                k = 3 * a + e
                xk = xe if a == 1 else pltpu.roll(xe, (WW * (1 - a)) % LANES, 1)
                xts[k, rows, :] = (xk * lmask[k:k + 1, :]).astype(BF)
        return 0

    lax.fori_loop(0, 8, shift, 0)

    def add_in(j, _):
        red_copy(j).wait_recv()
        own[...] += red_in[j].astype(F32)
        return 0

    lax.fori_loop(1, 8, add_in, 0)
    slope = slope_ref[...].astype(F32)
    weighted = slope * slope * curv_ref[...].astype(F32) * own[0:SHARE, :]
    weighted = jnp.concatenate([weighted, jnp.zeros((ROWS - SHARE, 128), F32)], axis=0)
    wgt[chan] = weighted.astype(BF)

    def wgt_copy(slot, n, dev):
        return remote(wgt.at[slot], wgt.at[slot], w_ss.at[n], w_rs.at[slot], dev)

    def spread(j, _):
        wgt_copy(chan, j, chip_dev(j)).start()
        return 0

    lax.fori_loop(1, 8, spread, 0)
    wgt_copy(chan, 0, sibling).start()

    def pass_on(j, _):
        slot = 2 * chip_at(-j) + core
        wgt_copy(slot, 0, sibling).wait_recv()
        wgt_copy(slot, 7 + j, sibling).start()
        return 0

    lax.fori_loop(1, 8, pass_on, 0)

    def from_sibling(j, _):
        wgt_copy(2 * chip_at(-j) + other, 0, sibling).wait_recv()
        return 0

    lax.fori_loop(0, 8, from_sibling, 0)

    def compact(c, _):
        w32[pl.ds(c * SHARE, 168), :] = wgt[c, 0:168, :].astype(F32)
        return 0

    lax.fori_loop(0, 16, compact, 0)
    w32[PIXELS:LANES, :] = jnp.zeros((LANES - PIXELS, 128), F32)

    def backward(t, _):
        rows = pl.ds(pl.multiple_of(t * BLOCK, 16), BLOCK)
        spot = pl.ds(pl.multiple_of(PAD + t * BLOCK, 16), BLOCK)
        w = w32[rows, :].astype(BF)
        w16[rows, :] = w
        for k in range(0, TAPS, 2):
            width = min(2, TAPS - k)
            kern = w_ref[k:k + width].reshape(128 * width, 128)
            res = lax.dot_general(w, kern, (((1,), (1,)), ((), ())), preferred_element_type=F32)
            for q in range(width):
                taps[k + q, spot, :] = res[:, 128 * q:128 * q + 128]
        return 0

    lax.fori_loop(0, LANES // BLOCK, backward, 0)

    def cx_copy(j):
        return remote(cx_out.at[j], cx_in.at[j], x_ss.at[j], x_rs.at[j], across)

    def cz_copy(j):
        return remote(cz_out.at[j], cz_in.at[j], d_ss.at[j], d_rs.at[j], z_dev(j))

    def to_across(j, _):
        j = lax.rem(j + 1, 8)

        def put(s, n, acc):
            cx_out[j, s:s + n, :] = acc.astype(BF)

        combined(theirs + at_z(j), True, put)
        cx_copy(j).start()
        return 0

    lax.fori_loop(0, 8, to_across, 0)

    def to_z(j, _):
        cx_copy(j).wait_recv()

        def put(s, n, acc):
            cz_out[j, s:s + n, :] = (acc + cx_in[j, s:s + n, :].astype(F32)).astype(BF)

        combined(mine + at_z(j), True, put)
        cz_copy(j).start()
        return 0

    lax.fori_loop(1, 8, to_z, 0)
    cx_copy(0).wait_recv()

    def put_last(s, n, acc):
        own[s:s + n, :] = acc + cx_in[0, s:s + n, :].astype(F32)

    combined(mine + z, True, put_last)

    scale = F32(1.0) / jnp.sqrt(F32(PIXELS))

    def product(k, _):
        res = jnp.dot(xts[k], w16[...], preferred_element_type=F32)
        kp_ref[k] = res * scale
        return 0

    lax.fori_loop(0, TAPS, product, 0)

    def add_z(j, _):
        cz_copy(j).wait_recv()
        own[...] += cz_in[j].astype(F32)
        return 0

    lax.fori_loop(1, 8, add_z, 0)
    cot_ref[...] = own[0:SHARE, :].astype(BF)

    for c in sent:
        c.wait_send()

    def drain(j, _):
        sib_copy(j).wait_send()
        cx_copy(j).wait_send()
        wgt_copy(chan, j, sibling).wait_send()
        return 0

    lax.fori_loop(0, 8, drain, 0)

    def drain_far(j, _):
        red_copy(j).wait_send()
        cz_copy(j).wait_send()
        wgt_copy(chan, 7 + j, sibling).wait_send()
        return 0

    lax.fori_loop(1, 8, drain_far, 0)


def per_device(activations, act_tangent, kernel, kernel_tangent, slope, curvature):
    vm = pl.BlockSpec(memory_space=pltpu.VMEM)
    dma = pltpu.SemaphoreType.DMA
    share = (8, ROWS, 128)
    return pl.pallas_call(
        body,
        out_shape=(
            jax.ShapeDtypeStruct((SHARE, 128), BF),
            jax.ShapeDtypeStruct((TAPS, 128, 128), F32),
        ),
        in_specs=[vm] * 8,
        out_specs=(vm, vm),
        scratch_shapes=[
            pltpu.VMEM((16, 16, LANES), BF),
            pltpu.VMEM((256, TAPS * 128), BF),
            pltpu.VMEM((TAPS, PAD + LANES, 128), F32),
            pltpu.VMEM((TAPS, 128, LANES), BF),
            pltpu.VMEM((PAD + LANES, 128), F32),
            pltpu.VMEM((LANES, 128), BF),
            pltpu.VMEM(share, F32),
            pltpu.VMEM(share, F32),
            pltpu.VMEM(share, BF),
            pltpu.VMEM(share, BF),
            pltpu.VMEM((ROWS, 128), F32),
            pltpu.VMEM((16, ROWS, 128), BF),
            pltpu.VMEM(share, BF),
            pltpu.VMEM(share, BF),
            pltpu.VMEM(share, BF),
            pltpu.VMEM(share, BF),
            dma((24,)), dma((16,)), dma((16,)),
            dma((8,)), dma((8,)), dma((8,)), dma((8,)),
            dma((16,)), dma((16,)), dma((8,)), dma((8,)), dma((8,)), dma((8,)),
        ],
        compiler_params=pltpu.CompilerParams(
            collective_id=0, has_side_effects=True, vmem_limit_bytes=56 * 1024 * 1024
        ),
        name="gauss_newton",
    )(
        activations.T, act_tangent.T, kernel, kernel_tangent, slope, curvature,
        jnp.asarray(row_masks()), jnp.asarray(lane_masks()),
    )


def solution(mesh):
    return jax.shard_map(
        per_device,
        mesh=mesh,
        in_specs=(
            P(None, ("chan", "filt")),
            P(None, ("chan", "filt")),
            P(None, "chan", "filt"),
            P(None, "chan", "filt"),
            P("chan", "filt"),
            P("chan", "filt"),
        ),
        out_specs=(P("filt", "chan"), P(None, "chan", "filt")),
        check_vma=False,
    )
```

```python
import jax
import jax.numpy as jnp
import numpy as np
from jax import lax
from jax.experimental import pallas as pl
from jax.experimental.pallas import tpu as pltpu
from jax.sharding import PartitionSpec as P

HH = 12
WW = 12
IMAGE = HH * WW
PIXELS = 2592
LANES = 2688
CUT = 1152
SHARE = 162
ROWS = 176
PAD = 16
BLOCK = 384
TAPS = 9
BF = jnp.bfloat16
F32 = jnp.float32


def row_masks():
    r = np.arange(IMAGE + ROWS)
    i, j = (r // WW) % HH, r % WW
    m = np.stack([i >= 1, i <= HH - 2, j >= 1, j <= WW - 2]).astype(np.float32)
    return np.ascontiguousarray(np.broadcast_to(m[:, :, None], (*m.shape, 128)))


def lane_masks():
    p = np.arange(LANES)
    i, j = (p // WW) % HH, p % WW
    m = np.zeros((16, LANES), np.float32)
    for a in range(3):
        for e in range(3):
            si, sj = i + a - 1, j + e - 1
            m[3 * a + e] = (si >= 0) & (si < HH) & (sj >= 0) & (sj < WW) & (p < PIXELS)
    return m


def body(
    acts_ref, tans_ref, w_ref, v_ref, slope_ref, curv_ref, rmask, lmask,
    cot_ref, kp_ref,
    gath, wcat, taps, xts, w32, w16, sib_out, sib_in, red_out, red_in, own,
    wgt, cx_out, cx_in, cz_out, cz_in,
    a_ss, lo_rs, hi_rs, s_ss, s_rs, b_ss, b_rs, w_ss, w_rs, x_ss, x_rs, d_ss, d_rs,
):
    chan = lax.axis_index("chan")
    filt = lax.axis_index("filt")
    core = lax.rem(chan, 2)
    chip = lax.div(chan, 2)
    half = lax.div(filt, 8)
    z = lax.rem(filt, 8)
    other = 1 - core
    sibling = {"chan": 2 * chip + other, "filt": filt}
    across = {"chan": chan, "filt": (1 - half) * 8 + z}

    def at_z(d):
        return lax.rem(z + d + 8, 8)

    def z_dev(d):
        return {"chan": chan, "filt": half * 8 + at_z(d)}

    def chip_at(j, sign=1):
        row = lax.rem(lax.div(chip, 2) + sign * lax.div(j, 2) + 4, 4)
        return 2 * row + lax.rem(chip + j, 2)

    def chip_dev(j):
        return {"chan": 2 * chip_at(j) + core, "filt": filt}

    def turns(i, middle):
        return middle + (1 - 2 * lax.rem(i, 2)) * lax.div(i + 1, 2)

    def chip_turn(i):
        return 2 * turns(lax.rem(i, 4), 2) + 1 - lax.div(i, 4)

    def z_turn(i):
        return turns(i, 4)

    def remote(src, dst, ss, rs, dev):
        return pltpu.make_async_remote_copy(
            src_ref=src, dst_ref=dst, send_sem=ss, recv_sem=rs,
            device_id=dev, device_id_type=pl.DeviceIdType.MESH,
        )

    barrier = pltpu.get_barrier_semaphore()
    peers = [sibling, across]
    peers += [z_dev(d) for d in range(1, 8)] + [chip_dev(jnp.int32(d)) for d in range(1, 8)]
    for dev in peers:
        pl.semaphore_signal(barrier, inc=1, device_id=dev, device_id_type=pl.DeviceIdType.MESH)

    both = jnp.concatenate([acts_ref[...].astype(F32), tans_ref[...].astype(F32)], axis=0)
    both = jnp.concatenate([both, jnp.zeros((16, LANES - PIXELS), F32)], axis=1)
    gath[filt] = both.astype(BF)
    pl.semaphore_wait(barrier, len(peers))

    mine = half * 8
    theirs = (1 - half) * 8
    right, left = z_dev(1), z_dev(-1)
    sent = []
    LOW, HIGH = pl.ds(0, CUT), pl.ds(CUT, LANES - CUT)

    def piece(slot, lanes, n, dev):
        ref = gath.at[slot, :, lanes]
        sem = lo_rs if lanes is LOW else hi_rs
        return remote(ref, ref, a_ss.at[n], sem.at[slot], dev)

    def send(slot, lanes, *devs):
        for dev in devs:
            c = piece(slot, lanes, len(sent), dev)
            c.start()
            sent.append(c)

    def got(slot, lanes):
        piece(slot, lanes, 0, across).wait_recv()

    send(filt, LOW, across)
    send(filt, HIGH, right, left)
    send(filt, LOW, right, left)
    send(filt, HIGH, across)

    for k in range(TAPS):
        vk = v_ref[k].astype(F32).reshape(16, 1, 8, 128)
        wk = w_ref[k].astype(F32).reshape(16, 1, 8, 128)
        wcat[:, 128 * k:128 * k + 128] = (
            jnp.concatenate([vk, wk], axis=1).reshape(256, 128).astype(BF)
        )
        taps[k, 0:PAD, :] = jnp.zeros((PAD, 128), F32)

    got(theirs + z, LOW)
    send(theirs + z, LOW, right, left)
    for h in range(1, 5):
        slot = mine + at_z(-h)
        got(slot, HIGH)
        if h < 4:
            send(slot, HIGH, right)
        send(slot, HIGH, across)
        if h < 4:
            slot = mine + at_z(h)
            got(slot, HIGH)
            if h < 3:
                send(slot, HIGH, left)
            send(slot, HIGH, across)
        for group in (mine, theirs):
            slot = group + at_z(h)
            got(slot, LOW)
            if h < 4:
                send(slot, LOW, left)
                slot = group + at_z(-h)
                got(slot, LOW)
                if h < 3:
                    send(slot, LOW, right)

    def forward(t, _):
        lanes = pl.ds(pl.multiple_of(t * BLOCK, 128), BLOCK)
        rows = pl.ds(pl.multiple_of(PAD + t * BLOCK, 16), BLOCK)
        x = gath[:, :, lanes].reshape(256, BLOCK).T
        for k in range(0, TAPS, 2):
            width = min(2, TAPS - k)
            res = jnp.dot(x, wcat[:, 128 * k:128 * (k + width)], preferred_element_type=F32)
            for q in range(width):
                taps[k + q, rows, :] = res[:, 128 * q:128 * q + 128]
        return 0

    lax.fori_loop(0, CUT // BLOCK, forward, 0)
    got(theirs + z, HIGH)
    for h in range(1, 8):
        got(theirs + at_z(h), HIGH)
    lax.fori_loop(CUT // BLOCK, LANES // BLOCK, forward, 0)

    def combined(c, flip, put):
        start = c * SHARE
        within = lax.rem(start, IMAGE)
        step = ROWS // 2
        for s in range(0, ROWS, step):
            m = [rmask[n, pl.ds(within + s, step), :] for n in range(4)]
            acc = None
            for a in range(3):
                part = None
                for e in range(3):
                    k = 3 * a + e
                    off = WW * (a - 1) + e - 1
                    val = taps[8 - k if flip else k, pl.ds(PAD + start + s + off, step), :]
                    if e == 0:
                        val = val * m[2]
                    if e == 2:
                        val = val * m[3]
                    part = val if part is None else part + val
                if a == 0:
                    part = part * m[0]
                if a == 2:
                    part = part * m[1]
                acc = part if acc is None else acc + part
            put(s, step, acc)

    def sib_copy(d):
        return remote(sib_out.at[d], sib_in.at[d], s_ss.at[d], s_rs.at[d], sibling)

    def to_sibling(j, _):
        d = chip_at(chip_turn(j))

        def put(s, n, acc):
            sib_out[d, s:s + n, :] = acc

        combined(2 * d + other, False, put)
        sib_copy(d).start()
        return 0

    lax.fori_loop(0, 8, to_sibling, 0)

    def red_copy(j):
        d = chip_at(j)
        return remote(red_out.at[j], red_in.at[j], b_ss.at[j], b_rs.at[j], chip_dev(j))

    def to_chip(i, _):
        j = chip_turn(i)
        d = chip_at(j)
        sib_copy(d).wait_recv()

        def put(s, n, acc):
            red_out[j, s:s + n, :] = (acc + sib_in[d, s:s + n, :]).astype(BF)

        combined(2 * d + core, False, put)
        red_copy(j).start()
        return 0

    lax.fori_loop(0, 7, to_chip, 0)
    sib_copy(chip).wait_recv()

    def put_own(s, n, acc):
        own[s:s + n, :] = acc + sib_in[chip, s:s + n, :]

    combined(2 * chip + core, False, put_own)

    def shift(t, _):
        g = gath[pl.ds(2 * t, 2)].astype(F32)
        x = g[:, 0:8, :].reshape(16, LANES)
        rows = pl.ds(pl.multiple_of(16 * t, 16), 16)
        for e in range(3):
            xe = x if e == 1 else pltpu.roll(x, (1 - e) % LANES, 1)
            for a in range(3):
                k = 3 * a + e
                xk = xe if a == 1 else pltpu.roll(xe, (WW * (1 - a)) % LANES, 1)
                xts[k, rows, :] = (xk * lmask[k:k + 1, :]).astype(BF)
        return 0

    lax.fori_loop(0, 8, shift, 0)

    def add_in(i, _):
        j = chip_turn(i)
        red_copy(j).wait_recv()
        own[...] += red_in[j].astype(F32)
        return 0

    lax.fori_loop(0, 7, add_in, 0)
    slope = slope_ref[...].astype(F32)
    weighted = slope * slope * curv_ref[...].astype(F32) * own[0:SHARE, :]
    weighted = jnp.concatenate([weighted, jnp.zeros((ROWS - SHARE, 128), F32)], axis=0)
    wgt[chan] = weighted.astype(BF)

    def wgt_copy(slot, n, dev):
        return remote(wgt.at[slot], wgt.at[slot], w_ss.at[n], w_rs.at[slot], dev)

    def spread(i, _):
        j = chip_turn(i)
        wgt_copy(chan, j, chip_dev(j)).start()
        return 0

    lax.fori_loop(0, 7, spread, 0)
    wgt_copy(chan, 0, sibling).start()

    def pass_on(i, _):
        j = chip_turn(i)
        slot = 2 * chip_at(j, -1) + core
        wgt_copy(slot, 0, sibling).wait_recv()
        wgt_copy(slot, 7 + j, sibling).start()
        return 0

    lax.fori_loop(0, 7, pass_on, 0)

    def from_sibling(j, _):
        wgt_copy(2 * chip_at(j) + other, 0, sibling).wait_recv()
        return 0

    lax.fori_loop(0, 8, from_sibling, 0)

    def compact(c, _):
        w32[pl.ds(c * SHARE, 168), :] = wgt[c, 0:168, :].astype(F32)
        return 0

    lax.fori_loop(0, 16, compact, 0)
    w32[PIXELS:LANES, :] = jnp.zeros((LANES - PIXELS, 128), F32)

    def backward(t, _):
        rows = pl.ds(pl.multiple_of(t * BLOCK, 16), BLOCK)
        spot = pl.ds(pl.multiple_of(PAD + t * BLOCK, 16), BLOCK)
        w = w32[rows, :].astype(BF)
        w16[rows, :] = w
        for k in range(0, TAPS, 2):
            width = min(2, TAPS - k)
            kern = w_ref[k:k + width].reshape(128 * width, 128)
            res = lax.dot_general(w, kern, (((1,), (1,)), ((), ())), preferred_element_type=F32)
            for q in range(width):
                taps[k + q, spot, :] = res[:, 128 * q:128 * q + 128]
        return 0

    lax.fori_loop(0, LANES // BLOCK, backward, 0)

    def cx_copy(j):
        return remote(cx_out.at[j], cx_in.at[j], x_ss.at[j], x_rs.at[j], across)

    def cz_copy(j):
        return remote(cz_out.at[j], cz_in.at[j], d_ss.at[j], d_rs.at[j], z_dev(j))

    def to_across(i, _):
        j = z_turn(i)

        def put(s, n, acc):
            cx_out[j, s:s + n, :] = acc.astype(BF)

        combined(theirs + at_z(j), True, put)
        cx_copy(j).start()
        return 0

    lax.fori_loop(0, 8, to_across, 0)

    def to_z(i, _):
        j = z_turn(i)
        cx_copy(j).wait_recv()

        def put(s, n, acc):
            cz_out[j, s:s + n, :] = (acc + cx_in[j, s:s + n, :].astype(F32)).astype(BF)

        combined(mine + at_z(j), True, put)
        cz_copy(j).start()
        return 0

    lax.fori_loop(0, 7, to_z, 0)
    cx_copy(0).wait_recv()

    def put_last(s, n, acc):
        own[s:s + n, :] = acc + cx_in[0, s:s + n, :].astype(F32)

    combined(mine + z, True, put_last)

    scale = F32(1.0) / jnp.sqrt(F32(PIXELS))

    def product(k, _):
        res = jnp.dot(xts[k], w16[...], preferred_element_type=F32)
        kp_ref[k] = res * scale
        return 0

    lax.fori_loop(0, TAPS, product, 0)

    def add_z(i, _):
        j = z_turn(i)
        cz_copy(j).wait_recv()
        own[...] += cz_in[j].astype(F32)
        return 0

    lax.fori_loop(0, 7, add_z, 0)
    cot_ref[...] = own[0:SHARE, :].astype(BF)

    for c in sent:
        c.wait_send()

    def drain(j, _):
        sib_copy(j).wait_send()
        cx_copy(j).wait_send()
        wgt_copy(chan, j, sibling).wait_send()
        return 0

    lax.fori_loop(0, 8, drain, 0)

    def drain_far(j, _):
        red_copy(j).wait_send()
        cz_copy(j).wait_send()
        wgt_copy(chan, 7 + j, sibling).wait_send()
        return 0

    lax.fori_loop(1, 8, drain_far, 0)


def per_device(activations, act_tangent, kernel, kernel_tangent, slope, curvature):
    vm = pl.BlockSpec(memory_space=pltpu.VMEM)
    dma = pltpu.SemaphoreType.DMA
    share = (8, ROWS, 128)
    return pl.pallas_call(
        body,
        out_shape=(
            jax.ShapeDtypeStruct((SHARE, 128), BF),
            jax.ShapeDtypeStruct((TAPS, 128, 128), F32),
        ),
        in_specs=[vm] * 8,
        out_specs=(vm, vm),
        scratch_shapes=[
            pltpu.VMEM((16, 16, LANES), BF),
            pltpu.VMEM((256, TAPS * 128), BF),
            pltpu.VMEM((TAPS, PAD + LANES, 128), F32),
            pltpu.VMEM((TAPS, 128, LANES), BF),
            pltpu.VMEM((PAD + LANES, 128), F32),
            pltpu.VMEM((LANES, 128), BF),
            pltpu.VMEM(share, F32),
            pltpu.VMEM(share, F32),
            pltpu.VMEM(share, BF),
            pltpu.VMEM(share, BF),
            pltpu.VMEM((ROWS, 128), F32),
            pltpu.VMEM((16, ROWS, 128), BF),
            pltpu.VMEM(share, BF),
            pltpu.VMEM(share, BF),
            pltpu.VMEM(share, BF),
            pltpu.VMEM(share, BF),
            dma((32,)), dma((16,)), dma((16,)),
            dma((8,)), dma((8,)), dma((8,)), dma((8,)),
            dma((16,)), dma((16,)), dma((8,)), dma((8,)), dma((8,)), dma((8,)),
        ],
        compiler_params=pltpu.CompilerParams(
            collective_id=0, has_side_effects=True, vmem_limit_bytes=56 * 1024 * 1024
        ),
        name="gauss_newton",
    )(
        activations.T, act_tangent.T, kernel, kernel_tangent, slope, curvature,
        jnp.asarray(row_masks()), jnp.asarray(lane_masks()),
    )


def solution(mesh):
    return jax.shard_map(
        per_device,
        mesh=mesh,
        in_specs=(
            P(None, ("chan", "filt")),
            P(None, ("chan", "filt")),
            P(None, "chan", "filt"),
            P(None, "chan", "filt"),
            P("chan", "filt"),
            P("chan", "filt"),
        ),
        out_specs=(P("filt", "chan"), P(None, "chan", "filt")),
        check_vma=False,
    )
```

```python
import jax
import jax.numpy as jnp
import numpy as np
from jax import lax
from jax.experimental import pallas as pl
from jax.experimental.pallas import tpu as pltpu
from jax.sharding import PartitionSpec as P

HH = 12
WW = 12
IMAGE = HH * WW
PIXELS = 2592
LANES = 2688
CUT = 1152
SHARE = 162
ROWS = 176
PAD = 16
BLOCK = 384
TAPS = 9
BF = jnp.bfloat16
F32 = jnp.float32


def row_masks():
    r = np.arange(IMAGE + ROWS)
    i, j = (r // WW) % HH, r % WW
    m = np.stack([i >= 1, i <= HH - 2, j >= 1, j <= WW - 2]).astype(np.float32)
    return np.ascontiguousarray(np.broadcast_to(m[:, :, None], (*m.shape, 128)))


def lane_masks():
    p = np.arange(LANES)
    i, j = (p // WW) % HH, p % WW
    m = np.zeros((16, LANES), np.float32)
    for a in range(3):
        for e in range(3):
            si, sj = i + a - 1, j + e - 1
            m[3 * a + e] = (si >= 0) & (si < HH) & (sj >= 0) & (sj < WW) & (p < PIXELS)
    return m


def body(
    acts_ref, tans_ref, w_hbm, v_hbm, slope_hbm, curv_hbm, rmask_hbm, lmask_hbm,
    cot_ref, kp_hbm,
    w_ref, v_ref, slope_ref, curv_ref, rmask, lmask, kp_ref,
    gath, wcat, taps, xts, w32, w16, sib_out, sib_in, red_out, red_in, own,
    wgt, cx_out, cx_in, cz_out, cz_in,
    l_s, k_s,
    a_ss, lo_rs, hi_rs, s_ss, s_rs, b_ss, b_rs, w_ss, w_rs, x_ss, x_rs, d_ss, d_rs,
):
    chan = lax.axis_index("chan")
    filt = lax.axis_index("filt")
    core = lax.rem(chan, 2)
    chip = lax.div(chan, 2)
    half = lax.div(filt, 8)
    z = lax.rem(filt, 8)
    other = 1 - core
    sibling = {"chan": 2 * chip + other, "filt": filt}
    across = {"chan": chan, "filt": (1 - half) * 8 + z}

    def at_z(d):
        return lax.rem(z + d + 8, 8)

    def z_dev(d):
        return {"chan": chan, "filt": half * 8 + at_z(d)}

    def diag_dev(d):
        return {"chan": chan, "filt": (1 - half) * 8 + at_z(d)}

    def chip_at(j, sign=1):
        row = lax.rem(lax.div(chip, 2) + sign * lax.div(j, 2) + 4, 4)
        return 2 * row + lax.rem(chip + j, 2)

    def chip_dev(j):
        return {"chan": 2 * chip_at(j) + core, "filt": filt}

    def turns(i, middle):
        return middle + (1 - 2 * lax.rem(i, 2)) * lax.div(i + 1, 2)

    def chip_turn(i):
        return 2 * turns(lax.rem(i, 4), 2) + 1 - lax.div(i, 4)

    def z_turn(i):
        return turns(i, 4)

    def remote(src, dst, ss, rs, dev):
        return pltpu.make_async_remote_copy(
            src_ref=src, dst_ref=dst, send_sem=ss, recv_sem=rs,
            device_id=dev, device_id_type=pl.DeviceIdType.MESH,
        )

    barrier = pltpu.get_barrier_semaphore()
    peers = [sibling, across, diag_dev(1), diag_dev(-1)]
    peers += [z_dev(d) for d in range(1, 8)] + [chip_dev(jnp.int32(d)) for d in range(1, 8)]
    for dev in peers:
        pl.semaphore_signal(barrier, inc=1, device_id=dev, device_id_type=pl.DeviceIdType.MESH)

    pairs = [
        (v_hbm, v_ref), (w_hbm, w_ref), (rmask_hbm, rmask),
        (slope_hbm, slope_ref), (curv_hbm, curv_ref), (lmask_hbm, lmask),
    ]
    loads = [pltpu.make_async_copy(src, dst, l_s.at[n]) for n, (src, dst) in enumerate(pairs)]
    for c in loads:
        c.start()

    both = jnp.concatenate([acts_ref[...].astype(F32), tans_ref[...].astype(F32)], axis=0)
    both = jnp.concatenate([both, jnp.zeros((16, LANES - PIXELS), F32)], axis=1)
    gath[filt] = both.astype(BF)
    pl.semaphore_wait(barrier, len(peers))

    mine = half * 8
    theirs = (1 - half) * 8
    right, left = z_dev(1), z_dev(-1)
    sent = []
    LOW, HIGH = pl.ds(0, CUT), pl.ds(CUT, LANES - CUT)

    def piece(slot, lanes, n, dev):
        ref = gath.at[slot, :, lanes]
        sem = lo_rs if lanes is LOW else hi_rs
        return remote(ref, ref, a_ss.at[n], sem.at[slot], dev)

    def send(slot, lanes, *devs):
        for dev in devs:
            c = piece(slot, lanes, len(sent), dev)
            c.start()
            sent.append(c)

    def got(slot, lanes):
        piece(slot, lanes, 0, across).wait_recv()

    send(filt, LOW, diag_dev(1), diag_dev(-1))
    send(filt, HIGH, right, left)
    send(filt, LOW, right, left, across)
    send(filt, HIGH, across)

    for c in loads:
        c.wait()
    for k in range(TAPS):
        vk = v_ref[k].astype(F32).reshape(16, 1, 8, 128)
        wk = w_ref[k].astype(F32).reshape(16, 1, 8, 128)
        wcat[:, 128 * k:128 * k + 128] = (
            jnp.concatenate([vk, wk], axis=1).reshape(256, 128).astype(BF)
        )
        taps[k, 0:PAD, :] = jnp.zeros((PAD, 128), F32)

    for h in range(1, 5):
        slot = mine + at_z(-h)
        got(slot, HIGH)
        if h < 4:
            send(slot, HIGH, right)
            if h == 3:
                send(slot, HIGH, diag_dev(1))
            send(slot, HIGH, across)
            slot = mine + at_z(h)
            got(slot, HIGH)
            if h < 3:
                send(slot, HIGH, left)
            send(slot, HIGH, across)
        for group in (mine, theirs):
            slot = group + at_z(h)
            got(slot, LOW)
            if h < 4:
                send(slot, LOW, left)
                slot = group + at_z(-h)
                got(slot, LOW)
                if h < 3:
                    send(slot, LOW, right)

    got(theirs + z, LOW)

    def forward(t, _):
        lanes = pl.ds(pl.multiple_of(t * BLOCK, 128), BLOCK)
        rows = pl.ds(pl.multiple_of(PAD + t * BLOCK, 16), BLOCK)
        x = gath[:, :, lanes].reshape(256, BLOCK).T
        for k in range(0, TAPS, 2):
            width = min(2, TAPS - k)
            res = jnp.dot(x, wcat[:, 128 * k:128 * (k + width)], preferred_element_type=F32)
            for q in range(width):
                taps[k + q, rows, :] = res[:, 128 * q:128 * q + 128]
        return 0

    lax.fori_loop(0, CUT // BLOCK, forward, 0)
    got(theirs + z, HIGH)
    for h in range(1, 8):
        got(theirs + at_z(h), HIGH)
    lax.fori_loop(CUT // BLOCK, LANES // BLOCK, forward, 0)

    def combined(c, flip, put):
        start = c * SHARE
        within = lax.rem(start, IMAGE)
        step = ROWS // 2
        for s in range(0, ROWS, step):
            m = [rmask[n, pl.ds(within + s, step), :] for n in range(4)]
            acc = None
            for a in range(3):
                part = None
                for e in range(3):
                    k = 3 * a + e
                    off = WW * (a - 1) + e - 1
                    val = taps[8 - k if flip else k, pl.ds(PAD + start + s + off, step), :]
                    if e == 0:
                        val = val * m[2]
                    if e == 2:
                        val = val * m[3]
                    part = val if part is None else part + val
                if a == 0:
                    part = part * m[0]
                if a == 2:
                    part = part * m[1]
                acc = part if acc is None else acc + part
            put(s, step, acc)

    def sib_copy(d):
        return remote(sib_out.at[d], sib_in.at[d], s_ss.at[d], s_rs.at[d], sibling)

    def to_sibling(j, _):
        d = chip_at(chip_turn(j))

        def put(s, n, acc):
            sib_out[d, s:s + n, :] = acc

        combined(2 * d + other, False, put)
        sib_copy(d).start()
        return 0

    def red_copy(j):
        d = chip_at(j)
        return remote(red_out.at[j], red_in.at[j], b_ss.at[j], b_rs.at[j], chip_dev(j))

    def to_chip(i, _):
        j = chip_turn(i)
        d = chip_at(j)
        sib_copy(d).wait_recv()

        def put(s, n, acc):
            red_out[j, s:s + n, :] = (acc + sib_in[d, s:s + n, :]).astype(BF)

        combined(2 * d + core, False, put)
        red_copy(j).start()
        return 0

    def both_sends(i, _):
        to_sibling(i + 1, 0)
        to_chip(i, 0)
        return 0

    to_sibling(0, 0)
    lax.fori_loop(0, 7, both_sends, 0)
    sib_copy(chip).wait_recv()

    def put_own(s, n, acc):
        own[s:s + n, :] = acc + sib_in[chip, s:s + n, :]

    combined(2 * chip + core, False, put_own)

    def shift(t, _):
        g = gath[pl.ds(2 * t, 2)].astype(F32)
        x = g[:, 0:8, :].reshape(16, LANES)
        rows = pl.ds(pl.multiple_of(16 * t, 16), 16)
        for e in range(3):
            xe = x if e == 1 else pltpu.roll(x, (1 - e) % LANES, 1)
            for a in range(3):
                k = 3 * a + e
                xk = xe if a == 1 else pltpu.roll(xe, (WW * (1 - a)) % LANES, 1)
                xts[k, rows, :] = (xk * lmask[k:k + 1, :]).astype(BF)
        return 0

    lax.fori_loop(0, 8, shift, 0)

    def add_in(i, _):
        j = chip_turn(i)
        red_copy(j).wait_recv()
        own[...] += red_in[j].astype(F32)
        return 0

    lax.fori_loop(0, 7, add_in, 0)
    slope = slope_ref[...].astype(F32)
    weighted = slope * slope * curv_ref[...].astype(F32) * own[0:SHARE, :]
    weighted = jnp.concatenate([weighted, jnp.zeros((ROWS - SHARE, 128), F32)], axis=0)
    wgt[chan] = weighted.astype(BF)

    def wgt_copy(slot, n, dev):
        return remote(wgt.at[slot], wgt.at[slot], w_ss.at[n], w_rs.at[slot], dev)

    def spread(i, _):
        j = chip_turn(i)
        wgt_copy(chan, j, chip_dev(j)).start()
        return 0

    lax.fori_loop(0, 7, spread, 0)
    wgt_copy(chan, 0, sibling).start()

    def unpack(c):
        start = c * SHARE
        x = wgt[c].astype(F32)
        w32[pl.ds(start, 160), :] = x[0:160]
        w32[pl.ds(start + 160, 2), :] = x[160:162]

    def pass_on(i, _):
        j = chip_turn(i)
        slot = 2 * chip_at(j, -1) + core
        wgt_copy(slot, 0, sibling).wait_recv()
        wgt_copy(slot, 7 + j, sibling).start()
        unpack(slot)
        return 0

    unpack(chan)
    lax.fori_loop(0, 7, pass_on, 0)

    def from_sibling(i, _):
        slot = 2 * chip_at(chip_turn(lax.rem(i + 7, 8)), -1) + other
        wgt_copy(slot, 0, sibling).wait_recv()
        unpack(slot)
        return 0

    lax.fori_loop(0, 8, from_sibling, 0)
    w32[PIXELS:LANES, :] = jnp.zeros((LANES - PIXELS, 128), F32)

    def backward(i, _):
        t = lax.rem(i + 3 * (1 - half), LANES // BLOCK)
        rows = pl.ds(pl.multiple_of(t * BLOCK, 16), BLOCK)
        spot = pl.ds(pl.multiple_of(PAD + t * BLOCK, 16), BLOCK)
        w = w32[rows, :].astype(BF)
        w16[rows, :] = w
        for k in range(0, TAPS, 2):
            width = min(2, TAPS - k)
            kern = w_ref[k:k + width].reshape(128 * width, 128)
            res = lax.dot_general(w, kern, (((1,), (1,)), ((), ())), preferred_element_type=F32)
            for q in range(width):
                taps[k + q, spot, :] = res[:, 128 * q:128 * q + 128]
        return 0

    lax.fori_loop(0, 4, backward, 0)

    scale = F32(1.0) / jnp.sqrt(F32(PIXELS))

    def kp_copy(k):
        return pltpu.make_async_copy(kp_ref.at[k], kp_hbm.at[k], k_s.at[k])

    def product(k):
        kp_ref[k] = jnp.dot(xts[k], w16[...], preferred_element_type=F32) * scale
        kp_copy(k).start()

    def cx_copy(j):
        return remote(cx_out.at[j], cx_in.at[j], x_ss.at[j], x_rs.at[j], across)

    def cz_copy(j):
        return remote(cz_out.at[j], cz_in.at[j], d_ss.at[j], d_rs.at[j], z_dev(j))

    def to_across(i, _):
        j = z_turn(i)

        def put(s, n, acc):
            cx_out[j, s:s + n, :] = acc.astype(BF)

        combined(theirs + at_z(j), True, put)
        cx_copy(j).start()
        return 0

    lax.fori_loop(0, 8, to_across, 0)

    lax.fori_loop(4, LANES // BLOCK, backward, 0)

    def to_z(i, _):
        j = z_turn(i)
        cx_copy(j).wait_recv()

        def put(s, n, acc):
            cz_out[j, s:s + n, :] = (acc + cx_in[j, s:s + n, :].astype(F32)).astype(BF)

        combined(mine + at_z(j), True, put)
        cz_copy(j).start()
        product(i)
        return 0

    lax.fori_loop(0, 7, to_z, 0)
    cx_copy(0).wait_recv()

    def put_last(s, n, acc):
        own[s:s + n, :] = acc + cx_in[0, s:s + n, :].astype(F32)

    combined(mine + z, True, put_last)

    product(7)
    product(8)

    def add_z(i, _):
        j = z_turn(i)
        cz_copy(j).wait_recv()
        own[...] += cz_in[j].astype(F32)
        return 0

    lax.fori_loop(0, 7, add_z, 0)
    cot_ref[...] = own[0:SHARE, :].astype(BF)

    for c in sent:
        c.wait_send()
    for k in range(TAPS):
        kp_copy(k).wait()

    def drain(j, _):
        sib_copy(j).wait_send()
        cx_copy(j).wait_send()
        wgt_copy(chan, j, sibling).wait_send()
        return 0

    lax.fori_loop(0, 8, drain, 0)

    def drain_far(j, _):
        red_copy(j).wait_send()
        cz_copy(j).wait_send()
        wgt_copy(chan, 7 + j, sibling).wait_send()
        return 0

    lax.fori_loop(1, 8, drain_far, 0)


def settle(cot_in, kp_in, cot_ref, kp_ref, cot_v, kp_v, in_s, out_s):
    legs = [(cot_in, cot_v, cot_ref)]
    for n in range(3):
        part = pl.ds(3 * n, 3)
        legs.append((kp_in.at[part], kp_v.at[part], kp_ref.at[part]))
    for n, (src, via, _) in enumerate(legs):
        pltpu.make_async_copy(src, via, in_s.at[n]).start()
    for n, (src, via, dst) in enumerate(legs):
        pltpu.make_async_copy(src, via, in_s.at[n]).wait()
        pltpu.make_async_copy(via, dst, out_s.at[n]).start()
    for n, (_, via, dst) in enumerate(legs):
        pltpu.make_async_copy(via, dst, out_s.at[n]).wait()


def per_device(activations, act_tangent, kernel, kernel_tangent, slope, curvature):
    vm = pl.BlockSpec(memory_space=pltpu.VMEM)
    hbm = pl.BlockSpec(memory_space=pl.ANY)
    dma = pltpu.SemaphoreType.DMA
    share = (8, ROWS, 128)
    shapes = (
        jax.ShapeDtypeStruct((SHARE, 128), BF),
        jax.ShapeDtypeStruct((TAPS, 128, 128), F32),
    )
    results = pl.pallas_call(
        body,
        out_shape=shapes,
        in_specs=[vm] * 2 + [hbm] * 6,
        out_specs=(vm, hbm),
        scratch_shapes=[
            pltpu.VMEM((TAPS, 128, 128), BF),
            pltpu.VMEM((TAPS, 128, 128), BF),
            pltpu.VMEM((SHARE, 128), BF),
            pltpu.VMEM((SHARE, 128), BF),
            pltpu.VMEM((4, IMAGE + ROWS, 128), F32),
            pltpu.VMEM((16, LANES), F32),
            pltpu.VMEM((TAPS, 128, 128), F32),
            pltpu.VMEM((16, 16, LANES), BF),
            pltpu.VMEM((256, TAPS * 128), BF),
            pltpu.VMEM((TAPS, PAD + LANES, 128), F32),
            pltpu.VMEM((TAPS, 128, LANES), BF),
            pltpu.VMEM((PAD + LANES, 128), F32),
            pltpu.VMEM((LANES, 128), BF),
            pltpu.VMEM(share, F32),
            pltpu.VMEM(share, F32),
            pltpu.VMEM(share, BF),
            pltpu.VMEM(share, BF),
            pltpu.VMEM((ROWS, 128), F32),
            pltpu.VMEM((16, ROWS, 128), BF),
            pltpu.VMEM(share, BF),
            pltpu.VMEM(share, BF),
            pltpu.VMEM(share, BF),
            pltpu.VMEM(share, BF),
            dma((6,)), dma((TAPS,)),
            dma((34,)), dma((16,)), dma((16,)),
            dma((8,)), dma((8,)), dma((8,)), dma((8,)),
            dma((16,)), dma((16,)), dma((8,)), dma((8,)), dma((8,)), dma((8,)),
        ],
        compiler_params=pltpu.CompilerParams(
            collective_id=0, has_side_effects=True, vmem_limit_bytes=56 * 1024 * 1024
        ),
        name="gauss_newton",
    )(
        activations.T, act_tangent.T, kernel, kernel_tangent, slope, curvature,
        jnp.asarray(row_masks()), jnp.asarray(lane_masks()),
    )
    return pl.pallas_call(
        settle,
        out_shape=shapes,
        in_specs=[hbm, hbm],
        out_specs=(hbm, hbm),
        scratch_shapes=[
            pltpu.VMEM((SHARE, 128), BF), pltpu.VMEM((TAPS, 128, 128), F32), dma((4,)), dma((4,))
        ],
        name="settle",
    )(*results)


def solution(mesh):
    return jax.shard_map(
        per_device,
        mesh=mesh,
        in_specs=(
            P(None, ("chan", "filt")),
            P(None, ("chan", "filt")),
            P(None, "chan", "filt"),
            P(None, "chan", "filt"),
            P("chan", "filt"),
            P("chan", "filt"),
        ),
        out_specs=(P("filt", "chan"), P(None, "chan", "filt")),
        check_vma=False,
    )
```

```python
import jax
import jax.numpy as jnp
import numpy as np
from jax import lax
from jax.experimental import pallas as pl
from jax.experimental.pallas import tpu as pltpu
from jax.sharding import PartitionSpec as P

HH = 12
WW = 12
IMAGE = HH * WW
PIXELS = 2592
LANES = 2688
CUT = 1152
SHARE = 162
ROWS = 176
PARTS = ((0, 96), (96, 80))
PAD = 16
BLOCK = 384
TAPS = 9
BF = jnp.bfloat16
F32 = jnp.float32


def row_masks():
    r = np.arange(IMAGE + ROWS)
    i, j = (r // WW) % HH, r % WW
    m = np.stack([i >= 1, i <= HH - 2, j >= 1, j <= WW - 2]).astype(np.float32)
    return np.ascontiguousarray(np.broadcast_to(m[:, :, None], (*m.shape, 128)))


def lane_masks():
    p = np.arange(LANES)
    i, j = (p // WW) % HH, p % WW
    m = np.zeros((16, LANES), np.float32)
    for a in range(3):
        for e in range(3):
            si, sj = i + a - 1, j + e - 1
            m[3 * a + e] = (si >= 0) & (si < HH) & (sj >= 0) & (sj < WW) & (p < PIXELS)
    return m


def body(
    acts_ref, tans_ref, w_hbm, v_hbm, slope_hbm, curv_hbm, rmask_hbm, lmask_hbm,
    cot_ref, kp_hbm,
    w_ref, v_ref, slope_ref, curv_ref, rmask, lmask, kp_ref,
    gath, wcat, taps, xts, w32, w16, sib_out, sib_in, red_out, red_in, own,
    wgt, cx_out, cx_in, cz_out, cz_in,
    l_s, k_s,
    a_ss, lo_rs, hi_rs, s_ss, s_rs, b_ss, b_rs, w_ss, w_rs, x_ss, x_rs, d_ss, d_rs,
):
    chan = lax.axis_index("chan")
    filt = lax.axis_index("filt")
    core = lax.rem(chan, 2)
    chip = lax.div(chan, 2)
    half = lax.div(filt, 8)
    z = lax.rem(filt, 8)
    other = 1 - core
    sibling = {"chan": 2 * chip + other, "filt": filt}
    across = {"chan": chan, "filt": (1 - half) * 8 + z}

    def at_z(d):
        return lax.rem(z + d + 8, 8)

    def z_dev(d):
        return {"chan": chan, "filt": half * 8 + at_z(d)}

    def diag_dev(d):
        return {"chan": chan, "filt": (1 - half) * 8 + at_z(d)}

    def chip_at(j, sign=1):
        row = lax.rem(lax.div(chip, 2) + sign * lax.div(j, 2) + 4, 4)
        return 2 * row + lax.rem(chip + j, 2)

    def chip_dev(j):
        return {"chan": 2 * chip_at(j) + core, "filt": filt}

    def turns(i, middle):
        return middle + (1 - 2 * lax.rem(i, 2)) * lax.div(i + 1, 2)

    def chip_turn(i):
        return 2 * turns(lax.rem(i, 4), 2) + 1 - lax.div(i, 4)

    def z_turn(i):
        return turns(i, 4)

    def remote(src, dst, ss, rs, dev):
        return pltpu.make_async_remote_copy(
            src_ref=src, dst_ref=dst, send_sem=ss, recv_sem=rs,
            device_id=dev, device_id_type=pl.DeviceIdType.MESH,
        )

    barrier = pltpu.get_barrier_semaphore()
    peers = [sibling, across, diag_dev(1), diag_dev(-1)]
    peers += [z_dev(d) for d in range(1, 8)] + [chip_dev(jnp.int32(d)) for d in range(1, 8)]
    for dev in peers:
        pl.semaphore_signal(barrier, inc=1, device_id=dev, device_id_type=pl.DeviceIdType.MESH)

    pairs = [
        (v_hbm, v_ref), (w_hbm, w_ref), (rmask_hbm, rmask),
        (slope_hbm, slope_ref), (curv_hbm, curv_ref), (lmask_hbm, lmask),
    ]
    loads = [pltpu.make_async_copy(src, dst, l_s.at[n]) for n, (src, dst) in enumerate(pairs)]
    for c in loads:
        c.start()

    both = jnp.concatenate([acts_ref[...].astype(F32), tans_ref[...].astype(F32)], axis=0)
    both = jnp.concatenate([both, jnp.zeros((16, LANES - PIXELS), F32)], axis=1)
    gath[filt] = both.astype(BF)
    pl.semaphore_wait(barrier, len(peers))

    mine = half * 8
    theirs = (1 - half) * 8
    right, left = z_dev(1), z_dev(-1)
    sent = []
    LOW, HIGH = pl.ds(0, CUT), pl.ds(CUT, LANES - CUT)

    def piece(slot, lanes, n, dev):
        ref = gath.at[slot, :, lanes]
        sem = lo_rs if lanes is LOW else hi_rs
        return remote(ref, ref, a_ss.at[n], sem.at[slot], dev)

    def send(slot, lanes, *devs):
        for dev in devs:
            c = piece(slot, lanes, len(sent), dev)
            c.start()
            sent.append(c)

    def got(slot, lanes):
        piece(slot, lanes, 0, across).wait_recv()

    send(filt, LOW, diag_dev(1), diag_dev(-1))
    send(filt, HIGH, right, left)
    send(filt, LOW, right, left, across)
    send(filt, HIGH, across)

    for c in loads:
        c.wait()
    for k in range(TAPS):
        vk = v_ref[k].astype(F32).reshape(16, 1, 8, 128)
        wk = w_ref[k].astype(F32).reshape(16, 1, 8, 128)
        wcat[:, 128 * k:128 * k + 128] = (
            jnp.concatenate([vk, wk], axis=1).reshape(256, 128).astype(BF)
        )
        taps[k, 0:PAD, :] = jnp.zeros((PAD, 128), F32)

    for h in range(1, 5):
        slot = mine + at_z(-h)
        got(slot, HIGH)
        if h < 4:
            send(slot, HIGH, right)
            if h == 3:
                send(slot, HIGH, diag_dev(1))
            send(slot, HIGH, across)
            slot = mine + at_z(h)
            got(slot, HIGH)
            if h < 3:
                send(slot, HIGH, left)
            send(slot, HIGH, across)
        for group in (mine, theirs):
            slot = group + at_z(h)
            got(slot, LOW)
            if h < 4:
                send(slot, LOW, left)
                slot = group + at_z(-h)
                got(slot, LOW)
                if h < 3:
                    send(slot, LOW, right)

    got(theirs + z, LOW)

    def forward(t, _):
        lanes = pl.ds(pl.multiple_of(t * BLOCK, 128), BLOCK)
        rows = pl.ds(pl.multiple_of(PAD + t * BLOCK, 16), BLOCK)
        x = gath[:, :, lanes].reshape(256, BLOCK).T
        for k in range(0, TAPS, 2):
            width = min(2, TAPS - k)
            res = jnp.dot(x, wcat[:, 128 * k:128 * (k + width)], preferred_element_type=F32)
            for q in range(width):
                taps[k + q, rows, :] = res[:, 128 * q:128 * q + 128]
        return 0

    lax.fori_loop(0, CUT // BLOCK, forward, 0, unroll=True)
    got(theirs + z, HIGH)
    for h in range(1, 8):
        got(theirs + at_z(h), HIGH)
    lax.fori_loop(CUT // BLOCK, LANES // BLOCK, forward, 0, unroll=True)

    def combined(c, flip, part, put):
        start = c * SHARE
        within = lax.rem(start, IMAGE)
        first, count = PARTS[part]
        step = count // 2
        for s in range(first, first + count, step):
            m = [rmask[n, pl.ds(within + s, step), :] for n in range(4)]
            acc = None
            for a in range(3):
                row = None
                for e in range(3):
                    k = 3 * a + e
                    off = WW * (a - 1) + e - 1
                    val = taps[8 - k if flip else k, pl.ds(PAD + start + s + off, step), :]
                    if e == 0:
                        val = val * m[2]
                    if e == 2:
                        val = val * m[3]
                    row = val if row is None else row + val
                if a == 0:
                    row = row * m[0]
                if a == 2:
                    row = row * m[1]
                acc = row if acc is None else acc + row
            put(s, step, acc)

    def rows_of(part):
        return pl.ds(*PARTS[part])

    def sib_copy(d, part):
        return remote(
            sib_out.at[d, rows_of(part)], sib_in.at[d, rows_of(part)],
            s_ss.at[2 * d + part], s_rs.at[2 * d + part], sibling,
        )

    def to_sibling(i, part):
        d = chip_at(chip_turn(i))

        def put(s, n, acc):
            sib_out[d, s:s + n, :] = acc

        combined(2 * d + other, False, part, put)
        sib_copy(d, part).start()

    def red_copy(j, part):
        return remote(
            red_out.at[j, rows_of(part)], red_in.at[j, rows_of(part)],
            b_ss.at[2 * j + part], b_rs.at[2 * j + part], chip_dev(j),
        )

    def to_chip(i, part):
        j = chip_turn(i)
        d = chip_at(j)
        sib_copy(d, part).wait_recv()

        def put(s, n, acc):
            red_out[j, s:s + n, :] = (acc + sib_in[d, s:s + n, :]).astype(BF)

        combined(2 * d + core, False, part, put)
        red_copy(j, part).start()

    for part in range(2):

        def both_sends(i, _, part=part):
            to_sibling(i + 1, part)
            to_chip(i, part)
            return 0

        to_sibling(0, part)
        lax.fori_loop(0, 7, both_sends, 0)

    def put_own(s, n, acc):
        own[s:s + n, :] = acc + sib_in[chip, s:s + n, :]

    for part in range(2):
        sib_copy(chip, part).wait_recv()
        combined(2 * chip + core, False, part, put_own)

    def shift(t, _):
        g = gath[pl.ds(2 * t, 2)].astype(F32)
        x = g[:, 0:8, :].reshape(16, LANES)
        rows = pl.ds(pl.multiple_of(16 * t, 16), 16)
        for e in range(3):
            xe = x if e == 1 else pltpu.roll(x, (1 - e) % LANES, 1)
            for a in range(3):
                k = 3 * a + e
                xk = xe if a == 1 else pltpu.roll(xe, (WW * (1 - a)) % LANES, 1)
                xts[k, rows, :] = (xk * lmask[k:k + 1, :]).astype(BF)
        return 0

    lax.fori_loop(0, 4, shift, 0)

    def wgt_copy(slot, n, part, dev):
        ref = wgt.at[slot, rows_of(part)]
        return remote(ref, ref, w_ss.at[2 * n + part], w_rs.at[2 * slot + part], dev)

    for part, (first, count) in enumerate(PARTS):
        rows = slice(first, first + count)

        def add_in(i, _, part=part, rows=rows):
            j = chip_turn(i)
            red_copy(j, part).wait_recv()
            own[rows, :] += red_in[j, rows, :].astype(F32)
            return 0

        lax.fori_loop(0, 7, add_in, 0)
        valid = min(first + count, SHARE) - first
        slope = slope_ref[first:first + valid, :].astype(F32)
        curv = curv_ref[first:first + valid, :].astype(F32)
        weighted = slope * slope * curv * own[first:first + valid, :]
        if valid < count:
            weighted = jnp.concatenate([weighted, jnp.zeros((count - valid, 128), F32)], axis=0)
        wgt[chan, rows, :] = weighted.astype(BF)

        def spread(i, _, part=part):
            j = chip_turn(i)
            wgt_copy(chan, j, part, chip_dev(j)).start()
            return 0

        lax.fori_loop(0, 7, spread, 0)
        wgt_copy(chan, 0, part, sibling).start()

    lax.fori_loop(4, 8, shift, 0)

    def unpack(c, part):
        start = c * SHARE
        first, count = PARTS[part]
        x = wgt[c, rows_of(part), :].astype(F32)
        if part == 0:
            w32[pl.ds(start, 96), :] = x
        else:
            w32[pl.ds(start + 96, 64), :] = x[0:64]
            w32[pl.ds(start + 160, 2), :] = x[64:66]

    for part in range(2):

        def pass_on(i, _, part=part):
            j = chip_turn(i)
            slot = 2 * chip_at(j, -1) + core
            wgt_copy(slot, 0, part, sibling).wait_recv()
            wgt_copy(slot, 7 + j, part, sibling).start()
            unpack(slot, part)
            return 0

        unpack(chan, part)
        lax.fori_loop(0, 7, pass_on, 0)

    for part in range(2):

        def from_sibling(i, _, part=part):
            slot = 2 * chip_at(chip_turn(lax.rem(i + 7, 8)), -1) + other
            wgt_copy(slot, 0, part, sibling).wait_recv()
            unpack(slot, part)
            return 0

        lax.fori_loop(0, 8, from_sibling, 0)
    w32[PIXELS:LANES, :] = jnp.zeros((LANES - PIXELS, 128), F32)

    def backward(i, _):
        t = lax.rem(i + 3 * (1 - half), LANES // BLOCK)
        rows = pl.ds(pl.multiple_of(t * BLOCK, 16), BLOCK)
        spot = pl.ds(pl.multiple_of(PAD + t * BLOCK, 16), BLOCK)
        w = w32[rows, :].astype(BF)
        w16[rows, :] = w
        for k in range(0, TAPS, 2):
            width = min(2, TAPS - k)
            kern = w_ref[k:k + width].reshape(128 * width, 128)
            res = lax.dot_general(w, kern, (((1,), (1,)), ((), ())), preferred_element_type=F32)
            for q in range(width):
                taps[k + q, spot, :] = res[:, 128 * q:128 * q + 128]
        return 0

    lax.fori_loop(0, 4, backward, 0, unroll=True)

    scale = F32(1.0) / jnp.sqrt(F32(PIXELS))

    def kp_copy(k):
        return pltpu.make_async_copy(kp_ref.at[k], kp_hbm.at[k], k_s.at[k])

    def product(k):
        kp_ref[k] = jnp.dot(xts[k], w16[...], preferred_element_type=F32) * scale
        kp_copy(k).start()

    def cx_copy(j, part):
        return remote(
            cx_out.at[j, rows_of(part)], cx_in.at[j, rows_of(part)],
            x_ss.at[2 * j + part], x_rs.at[2 * j + part], across,
        )

    def cz_copy(j, part):
        return remote(
            cz_out.at[j, rows_of(part)], cz_in.at[j, rows_of(part)],
            d_ss.at[2 * j + part], d_rs.at[2 * j + part], z_dev(j),
        )

    def to_across(i, _):
        j = z_turn(i)

        def put(s, n, acc):
            cx_out[j, s:s + n, :] = acc.astype(BF)

        for part in range(2):
            combined(theirs + at_z(j), True, part, put)
            cx_copy(j, part).start()
        return 0

    lax.fori_loop(0, 8, to_across, 0)
    lax.fori_loop(4, LANES // BLOCK, backward, 0, unroll=True)

    def to_z(i, _):
        j = z_turn(i)

        def put(s, n, acc):
            cz_out[j, s:s + n, :] = (acc + cx_in[j, s:s + n, :].astype(F32)).astype(BF)

        for part in range(2):
            cx_copy(j, part).wait_recv()
            combined(mine + at_z(j), True, part, put)
            cz_copy(j, part).start()
        product(i)
        return 0

    lax.fori_loop(0, 7, to_z, 0)

    def put_last(s, n, acc):
        own[s:s + n, :] = acc + cx_in[0, s:s + n, :].astype(F32)

    for part in range(2):
        cx_copy(0, part).wait_recv()
        combined(mine + z, True, part, put_last)
    product(7)
    product(8)

    def add_z(i, _):
        j = z_turn(i)
        cz_copy(j, 0).wait_recv()
        cz_copy(j, 1).wait_recv()
        own[...] += cz_in[j].astype(F32)
        return 0

    lax.fori_loop(0, 7, add_z, 0)
    cot_ref[...] = own[0:SHARE, :].astype(BF)

    for c in sent:
        c.wait_send()
    for k in range(TAPS):
        kp_copy(k).wait()

    def drain(j, _):
        for part in range(2):
            sib_copy(j, part).wait_send()
            cx_copy(j, part).wait_send()
            wgt_copy(chan, j, part, sibling).wait_send()
        return 0

    lax.fori_loop(0, 8, drain, 0)

    def drain_far(j, _):
        for part in range(2):
            red_copy(j, part).wait_send()
            cz_copy(j, part).wait_send()
            wgt_copy(chan, 7 + j, part, sibling).wait_send()
        return 0

    lax.fori_loop(1, 8, drain_far, 0)


def settle(cot_in, kp_in, cot_ref, kp_ref, cot_v, kp_v, in_s, out_s):
    legs = [(cot_in, cot_v, cot_ref)]
    for n in range(3):
        part = pl.ds(3 * n, 3)
        legs.append((kp_in.at[part], kp_v.at[part], kp_ref.at[part]))
    for n, (src, via, _) in enumerate(legs):
        pltpu.make_async_copy(src, via, in_s.at[n]).start()
    for n, (src, via, dst) in enumerate(legs):
        pltpu.make_async_copy(src, via, in_s.at[n]).wait()
        pltpu.make_async_copy(via, dst, out_s.at[n]).start()
    for n, (_, via, dst) in enumerate(legs):
        pltpu.make_async_copy(via, dst, out_s.at[n]).wait()


def per_device(activations, act_tangent, kernel, kernel_tangent, slope, curvature):
    vm = pl.BlockSpec(memory_space=pltpu.VMEM)
    hbm = pl.BlockSpec(memory_space=pl.ANY)
    dma = pltpu.SemaphoreType.DMA
    share = (8, ROWS, 128)
    shapes = (
        jax.ShapeDtypeStruct((SHARE, 128), BF),
        jax.ShapeDtypeStruct((TAPS, 128, 128), F32),
    )
    results = pl.pallas_call(
        body,
        out_shape=shapes,
        in_specs=[vm] * 2 + [hbm] * 6,
        out_specs=(vm, hbm),
        scratch_shapes=[
            pltpu.VMEM((TAPS, 128, 128), BF),
            pltpu.VMEM((TAPS, 128, 128), BF),
            pltpu.VMEM((SHARE, 128), BF),
            pltpu.VMEM((SHARE, 128), BF),
            pltpu.VMEM((4, IMAGE + ROWS, 128), F32),
            pltpu.VMEM((16, LANES), F32),
            pltpu.VMEM((TAPS, 128, 128), F32),
            pltpu.VMEM((16, 16, LANES), BF),
            pltpu.VMEM((256, TAPS * 128), BF),
            pltpu.VMEM((TAPS, PAD + LANES, 128), F32),
            pltpu.VMEM((TAPS, 128, LANES), BF),
            pltpu.VMEM((PAD + LANES, 128), F32),
            pltpu.VMEM((LANES, 128), BF),
            pltpu.VMEM(share, F32),
            pltpu.VMEM(share, F32),
            pltpu.VMEM(share, BF),
            pltpu.VMEM(share, BF),
            pltpu.VMEM((ROWS, 128), F32),
            pltpu.VMEM((16, ROWS, 128), BF),
            pltpu.VMEM(share, BF),
            pltpu.VMEM(share, BF),
            pltpu.VMEM(share, BF),
            pltpu.VMEM(share, BF),
            dma((6,)), dma((TAPS,)),
            dma((34,)), dma((16,)), dma((16,)),
            dma((16,)), dma((16,)), dma((16,)), dma((16,)),
            dma((32,)), dma((32,)), dma((16,)), dma((16,)), dma((16,)), dma((16,)),
        ],
        compiler_params=pltpu.CompilerParams(
            collective_id=0, has_side_effects=True, vmem_limit_bytes=56 * 1024 * 1024
        ),
        name="gauss_newton",
    )(
        activations.T, act_tangent.T, kernel, kernel_tangent, slope, curvature,
        jnp.asarray(row_masks()), jnp.asarray(lane_masks()),
    )
    return pl.pallas_call(
        settle,
        out_shape=shapes,
        in_specs=[hbm, hbm],
        out_specs=(hbm, hbm),
        scratch_shapes=[
            pltpu.VMEM((SHARE, 128), BF), pltpu.VMEM((TAPS, 128, 128), F32), dma((4,)), dma((4,))
        ],
        name="settle",
    )(*results)


def solution(mesh):
    return jax.shard_map(
        per_device,
        mesh=mesh,
        in_specs=(
            P(None, ("chan", "filt")),
            P(None, ("chan", "filt")),
            P(None, "chan", "filt"),
            P(None, "chan", "filt"),
            P("chan", "filt"),
            P("chan", "filt"),
        ),
        out_specs=(P("filt", "chan"), P(None, "chan", "filt")),
        check_vma=False,
    )
```

```python
import jax
import jax.numpy as jnp
import numpy as np
from jax import lax
from jax.experimental import pallas as pl
from jax.experimental.pallas import tpu as pltpu
from jax.sharding import PartitionSpec as P

HH = 12
WW = 12
IMAGE = HH * WW
PIXELS = 2592
LANES = 2688
CUT = 1152
SHARE = 162
ROWS = 176
PARTS = ((0, 96), (96, 80))
PAD = 16
BLOCK = 384
TAPS = 9
BF = jnp.bfloat16
F32 = jnp.float32


def row_masks():
    r = np.arange(IMAGE + ROWS)
    i, j = (r // WW) % HH, r % WW
    m = np.stack([i >= 1, i <= HH - 2, j >= 1, j <= WW - 2]).astype(np.float32)
    return np.ascontiguousarray(np.broadcast_to(m[:, :, None], (*m.shape, 128)))


def lane_masks():
    p = np.arange(LANES)
    i, j = (p // WW) % HH, p % WW
    m = np.zeros((16, LANES), np.float32)
    for a in range(3):
        for e in range(3):
            si, sj = i + a - 1, j + e - 1
            m[3 * a + e] = (si >= 0) & (si < HH) & (sj >= 0) & (sj < WW) & (p < PIXELS)
    return m


def body(
    acts_ref, tans_ref, w_hbm, v_hbm, slope_hbm, curv_hbm, rmask_hbm, lmask_hbm,
    cot_ref, kp_hbm,
    w_ref, v_ref, slope_ref, curv_ref, rmask, lmask, kp_ref,
    gath, wcat, taps, xts, w32, w16, sib_out, sib_in, red_out, red_in, own,
    wgt, cx_out, cx_in, cz_out, cz_in,
    l_s, k_s,
    a_ss, lo_rs, hi_rs, s_ss, s_rs, b_ss, b_rs, w_ss, w_rs, x_ss, x_rs, d_ss, d_rs,
):
    chan = lax.axis_index("chan")
    filt = lax.axis_index("filt")
    core = lax.rem(chan, 2)
    chip = lax.div(chan, 2)
    half = lax.div(filt, 8)
    z = lax.rem(filt, 8)
    other = 1 - core
    sibling = {"chan": 2 * chip + other, "filt": filt}
    across = {"chan": chan, "filt": (1 - half) * 8 + z}

    def at_z(d):
        return lax.rem(z + d + 8, 8)

    def z_dev(d):
        return {"chan": chan, "filt": half * 8 + at_z(d)}

    def diag_dev(d):
        return {"chan": chan, "filt": (1 - half) * 8 + at_z(d)}

    def chip_at(j, sign=1):
        row = lax.rem(lax.div(chip, 2) + sign * lax.div(j, 2) + 4, 4)
        return 2 * row + lax.rem(chip + j, 2)

    def chip_dev(j):
        return {"chan": 2 * chip_at(j) + core, "filt": filt}

    def turns(i, middle):
        return middle + (1 - 2 * lax.rem(i, 2)) * lax.div(i + 1, 2)

    def chip_turn(i):
        return 2 * turns(lax.rem(i, 4), 2) + 1 - lax.div(i, 4)

    def z_turn(i):
        return turns(i, 4)

    def remote(src, dst, ss, rs, dev):
        return pltpu.make_async_remote_copy(
            src_ref=src, dst_ref=dst, send_sem=ss, recv_sem=rs,
            device_id=dev, device_id_type=pl.DeviceIdType.MESH,
        )

    barrier = pltpu.get_barrier_semaphore()
    peers = [sibling, across, diag_dev(1), diag_dev(-1)]
    peers += [z_dev(d) for d in range(1, 8)] + [chip_dev(jnp.int32(d)) for d in range(1, 8)]
    for dev in peers:
        pl.semaphore_signal(barrier, inc=1, device_id=dev, device_id_type=pl.DeviceIdType.MESH)

    pairs = [
        (v_hbm, v_ref), (w_hbm, w_ref), (rmask_hbm, rmask),
        (slope_hbm, slope_ref), (curv_hbm, curv_ref), (lmask_hbm, lmask),
    ]
    loads = [pltpu.make_async_copy(src, dst, l_s.at[n]) for n, (src, dst) in enumerate(pairs)]
    for c in loads:
        c.start()

    both = jnp.concatenate([acts_ref[...].astype(F32), tans_ref[...].astype(F32)], axis=0)
    both = jnp.concatenate([both, jnp.zeros((16, LANES - PIXELS), F32)], axis=1)
    gath[filt] = both.astype(BF)
    pl.semaphore_wait(barrier, len(peers))

    mine = half * 8
    theirs = (1 - half) * 8
    right, left = z_dev(1), z_dev(-1)
    sent = []
    LOW, HIGH = pl.ds(0, CUT), pl.ds(CUT, LANES - CUT)

    def piece(slot, lanes, n, dev):
        ref = gath.at[slot, :, lanes]
        sem = lo_rs if lanes is LOW else hi_rs
        return remote(ref, ref, a_ss.at[n], sem.at[slot], dev)

    def send(slot, lanes, *devs):
        for dev in devs:
            c = piece(slot, lanes, len(sent), dev)
            c.start()
            sent.append(c)

    def got(slot, lanes):
        piece(slot, lanes, 0, across).wait_recv()

    send(filt, LOW, diag_dev(1), diag_dev(-1))
    send(filt, HIGH, right, left)
    send(filt, LOW, right, left, across)
    send(filt, HIGH, across)

    for c in loads:
        c.wait()
    for k in range(TAPS):
        vk = v_ref[k].astype(F32).reshape(16, 1, 8, 128)
        wk = w_ref[k].astype(F32).reshape(16, 1, 8, 128)
        wcat[:, 128 * k:128 * k + 128] = (
            jnp.concatenate([vk, wk], axis=1).reshape(256, 128).astype(BF)
        )
        taps[k, 0:PAD, :] = jnp.zeros((PAD, 128), F32)

    for h in range(1, 5):
        slot = mine + at_z(-h)
        got(slot, HIGH)
        if h < 4:
            send(slot, HIGH, right)
            if h == 3:
                send(slot, HIGH, diag_dev(1))
            send(slot, HIGH, across)
            slot = mine + at_z(h)
            got(slot, HIGH)
            if h < 3:
                send(slot, HIGH, left)
            send(slot, HIGH, across)
        for group in (mine, theirs):
            slot = group + at_z(h)
            got(slot, LOW)
            if h < 4:
                send(slot, LOW, left)
                slot = group + at_z(-h)
                got(slot, LOW)
                if h < 3:
                    send(slot, LOW, right)

    got(theirs + z, LOW)

    def forward(t, _):
        lanes = pl.ds(pl.multiple_of(t * BLOCK, 128), BLOCK)
        rows = pl.ds(pl.multiple_of(PAD + t * BLOCK, 16), BLOCK)
        x = gath[:, :, lanes].reshape(256, BLOCK).T
        for k in range(0, TAPS, 2):
            width = min(2, TAPS - k)
            res = jnp.dot(x, wcat[:, 128 * k:128 * (k + width)], preferred_element_type=F32)
            for q in range(width):
                taps[k + q, rows, :] = res[:, 128 * q:128 * q + 128]
        return 0

    lax.fori_loop(0, CUT // BLOCK, forward, 0, unroll=True)
    got(theirs + z, HIGH)
    for h in range(1, 8):
        got(theirs + at_z(h), HIGH)
    lax.fori_loop(CUT // BLOCK, LANES // BLOCK, forward, 0, unroll=True)

    def combined(c, flip, part, put):
        start = c * SHARE
        within = lax.rem(start, IMAGE)
        first, count = PARTS[part]
        step = count // 2
        for s in range(first, first + count, step):
            m = [rmask[n, pl.ds(within + s, step), :] for n in range(4)]
            acc = None
            for a in range(3):
                row = None
                for e in range(3):
                    k = 3 * a + e
                    off = WW * (a - 1) + e - 1
                    val = taps[8 - k if flip else k, pl.ds(PAD + start + s + off, step), :]
                    if e == 0:
                        val = val * m[2]
                    if e == 2:
                        val = val * m[3]
                    row = val if row is None else row + val
                if a == 0:
                    row = row * m[0]
                if a == 2:
                    row = row * m[1]
                acc = row if acc is None else acc + row
            put(s, step, acc)

    def rows_of(part):
        return pl.ds(*PARTS[part])

    def sib_copy(d, part):
        return remote(
            sib_out.at[d, rows_of(part)], sib_in.at[d, rows_of(part)],
            s_ss.at[2 * d + part], s_rs.at[2 * d + part], sibling,
        )

    def to_sibling(i, part):
        d = chip_at(chip_turn(i))

        def put(s, n, acc):
            sib_out[d, s:s + n, :] = acc

        combined(2 * d + other, False, part, put)
        sib_copy(d, part).start()

    def red_copy(j, part):
        return remote(
            red_out.at[j, rows_of(part)], red_in.at[j, rows_of(part)],
            b_ss.at[2 * j + part], b_rs.at[2 * j + part], chip_dev(j),
        )

    def to_chip(i, part):
        j = chip_turn(i)
        d = chip_at(j)
        sib_copy(d, part).wait_recv()

        def put(s, n, acc):
            red_out[j, s:s + n, :] = (acc + sib_in[d, s:s + n, :]).astype(BF)

        combined(2 * d + core, False, part, put)
        red_copy(j, part).start()

    def ahead(first, last, part, step=None, chip_part=None):
        def go(i, _):
            to_sibling(i, part)
            if step is not None:
                to_chip(i + step, chip_part)
            return 0

        lax.fori_loop(first, last, go, 0)

    def behind(i, _):
        to_chip(i, 1)
        return 0

    ahead(0, 4, 0)
    ahead(4, 8, 0, -4, 0)
    ahead(0, 3, 1, 4, 0)
    ahead(3, 4, 1)
    ahead(4, 8, 1, -4, 1)
    lax.fori_loop(4, 7, behind, 0)

    def put_own(s, n, acc):
        own[s:s + n, :] = acc + sib_in[chip, s:s + n, :]

    for part in range(2):
        sib_copy(chip, part).wait_recv()
        combined(2 * chip + core, False, part, put_own)

    def shift(t, _):
        g = gath[pl.ds(2 * t, 2)].astype(F32)
        x = g[:, 0:8, :].reshape(16, LANES)
        rows = pl.ds(pl.multiple_of(16 * t, 16), 16)
        for e in range(3):
            xe = x if e == 1 else pltpu.roll(x, (1 - e) % LANES, 1)
            for a in range(3):
                k = 3 * a + e
                xk = xe if a == 1 else pltpu.roll(xe, (WW * (1 - a)) % LANES, 1)
                xts[k, rows, :] = (xk * lmask[k:k + 1, :]).astype(BF)
        return 0

    lax.fori_loop(0, 4, shift, 0)

    def wgt_copy(slot, n, part, dev):
        ref = wgt.at[slot, rows_of(part)]
        return remote(ref, ref, w_ss.at[2 * n + part], w_rs.at[2 * slot + part], dev)

    for part, (first, count) in enumerate(PARTS):
        rows = slice(first, first + count)

        def add_in(i, _, part=part, rows=rows):
            j = chip_turn(i)
            red_copy(j, part).wait_recv()
            own[rows, :] += red_in[j, rows, :].astype(F32)
            return 0

        lax.fori_loop(0, 7, add_in, 0)
        valid = min(first + count, SHARE) - first
        slope = slope_ref[first:first + valid, :].astype(F32)
        curv = curv_ref[first:first + valid, :].astype(F32)
        weighted = slope * slope * curv * own[first:first + valid, :]
        if valid < count:
            weighted = jnp.concatenate([weighted, jnp.zeros((count - valid, 128), F32)], axis=0)
        wgt[chan, rows, :] = weighted.astype(BF)

        def spread(i, _, part=part):
            j = chip_turn(i)
            wgt_copy(chan, j, part, chip_dev(j)).start()
            return 0

        lax.fori_loop(0, 7, spread, 0)
        wgt_copy(chan, 0, part, sibling).start()

    lax.fori_loop(4, 8, shift, 0)

    def unpack(c, part):
        start = c * SHARE
        first, count = PARTS[part]
        x = wgt[c, rows_of(part), :].astype(F32)
        if part == 0:
            w32[pl.ds(start, 96), :] = x
        else:
            w32[pl.ds(start + 96, 64), :] = x[0:64]
            w32[pl.ds(start + 160, 2), :] = x[64:66]

    for part in range(2):

        def pass_on(i, _, part=part):
            j = chip_turn(i)
            slot = 2 * chip_at(j, -1) + core
            wgt_copy(slot, 0, part, sibling).wait_recv()
            wgt_copy(slot, 7 + j, part, sibling).start()
            unpack(slot, part)
            return 0

        unpack(chan, part)
        lax.fori_loop(0, 7, pass_on, 0)

    for part in range(2):

        def from_sibling(i, _, part=part):
            slot = 2 * chip_at(chip_turn(lax.rem(i + 7, 8)), -1) + other
            wgt_copy(slot, 0, part, sibling).wait_recv()
            unpack(slot, part)
            return 0

        lax.fori_loop(0, 8, from_sibling, 0)
    w32[PIXELS:LANES, :] = jnp.zeros((LANES - PIXELS, 128), F32)

    def backward(i, _):
        t = lax.rem(i + 3 * (1 - half), LANES // BLOCK)
        rows = pl.ds(pl.multiple_of(t * BLOCK, 16), BLOCK)
        spot = pl.ds(pl.multiple_of(PAD + t * BLOCK, 16), BLOCK)
        w = w32[rows, :].astype(BF)
        w16[rows, :] = w
        for k in range(0, TAPS, 2):
            width = min(2, TAPS - k)
            kern = w_ref[k:k + width].reshape(128 * width, 128)
            res = lax.dot_general(w, kern, (((1,), (1,)), ((), ())), preferred_element_type=F32)
            for q in range(width):
                taps[k + q, spot, :] = res[:, 128 * q:128 * q + 128]
        return 0

    lax.fori_loop(0, 4, backward, 0, unroll=True)

    scale = F32(1.0) / jnp.sqrt(F32(PIXELS))

    def kp_copy(k):
        return pltpu.make_async_copy(kp_ref.at[k], kp_hbm.at[k], k_s.at[k])

    def product(k):
        kp_ref[k] = jnp.dot(xts[k], w16[...], preferred_element_type=F32) * scale
        kp_copy(k).start()

    def cx_copy(j, part):
        return remote(
            cx_out.at[j, rows_of(part)], cx_in.at[j, rows_of(part)],
            x_ss.at[2 * j + part], x_rs.at[2 * j + part], across,
        )

    def cz_copy(j, part):
        return remote(
            cz_out.at[j, rows_of(part)], cz_in.at[j, rows_of(part)],
            d_ss.at[2 * j + part], d_rs.at[2 * j + part], z_dev(j),
        )

    def to_across(i, _):
        j = z_turn(i)

        def put(s, n, acc):
            cx_out[j, s:s + n, :] = acc.astype(BF)

        for part in range(2):
            combined(theirs + at_z(j), True, part, put)
            cx_copy(j, part).start()
        return 0

    lax.fori_loop(0, 8, to_across, 0)
    lax.fori_loop(4, LANES // BLOCK, backward, 0, unroll=True)

    def to_z(i, _):
        j = z_turn(i)

        def put(s, n, acc):
            cz_out[j, s:s + n, :] = (acc + cx_in[j, s:s + n, :].astype(F32)).astype(BF)

        for part in range(2):
            cx_copy(j, part).wait_recv()
            combined(mine + at_z(j), True, part, put)
            cz_copy(j, part).start()
        product(i)
        return 0

    lax.fori_loop(0, 7, to_z, 0)

    def put_last(s, n, acc):
        own[s:s + n, :] = acc + cx_in[0, s:s + n, :].astype(F32)

    for part in range(2):
        cx_copy(0, part).wait_recv()
        combined(mine + z, True, part, put_last)
    product(7)
    product(8)

    def add_z(i, _):
        j = z_turn(i)
        cz_copy(j, 0).wait_recv()
        cz_copy(j, 1).wait_recv()
        own[...] += cz_in[j].astype(F32)
        return 0

    lax.fori_loop(0, 7, add_z, 0)
    cot_ref[...] = own[0:SHARE, :].astype(BF)

    for c in sent:
        c.wait_send()
    for k in range(TAPS):
        kp_copy(k).wait()

    def drain(j, _):
        for part in range(2):
            sib_copy(j, part).wait_send()
            cx_copy(j, part).wait_send()
            wgt_copy(chan, j, part, sibling).wait_send()
        return 0

    lax.fori_loop(0, 8, drain, 0)

    def drain_far(j, _):
        for part in range(2):
            red_copy(j, part).wait_send()
            cz_copy(j, part).wait_send()
            wgt_copy(chan, 7 + j, part, sibling).wait_send()
        return 0

    lax.fori_loop(1, 8, drain_far, 0)


def settle(cot_in, kp_in, cot_ref, kp_ref, cot_v, kp_v, in_s, out_s):
    legs = [(cot_in, cot_v, cot_ref)]
    for n in range(3):
        part = pl.ds(3 * n, 3)
        legs.append((kp_in.at[part], kp_v.at[part], kp_ref.at[part]))
    for n, (src, via, _) in enumerate(legs):
        pltpu.make_async_copy(src, via, in_s.at[n]).start()
    for n, (src, via, dst) in enumerate(legs):
        pltpu.make_async_copy(src, via, in_s.at[n]).wait()
        pltpu.make_async_copy(via, dst, out_s.at[n]).start()
    for n, (_, via, dst) in enumerate(legs):
        pltpu.make_async_copy(via, dst, out_s.at[n]).wait()


def per_device(activations, act_tangent, kernel, kernel_tangent, slope, curvature):
    vm = pl.BlockSpec(memory_space=pltpu.VMEM)
    hbm = pl.BlockSpec(memory_space=pl.ANY)
    dma = pltpu.SemaphoreType.DMA
    share = (8, ROWS, 128)
    shapes = (
        jax.ShapeDtypeStruct((SHARE, 128), BF),
        jax.ShapeDtypeStruct((TAPS, 128, 128), F32),
    )
    results = pl.pallas_call(
        body,
        out_shape=shapes,
        in_specs=[vm] * 2 + [hbm] * 6,
        out_specs=(vm, hbm),
        scratch_shapes=[
            pltpu.VMEM((TAPS, 128, 128), BF),
            pltpu.VMEM((TAPS, 128, 128), BF),
            pltpu.VMEM((SHARE, 128), BF),
            pltpu.VMEM((SHARE, 128), BF),
            pltpu.VMEM((4, IMAGE + ROWS, 128), F32),
            pltpu.VMEM((16, LANES), F32),
            pltpu.VMEM((TAPS, 128, 128), F32),
            pltpu.VMEM((16, 16, LANES), BF),
            pltpu.VMEM((256, TAPS * 128), BF),
            pltpu.VMEM((TAPS, PAD + LANES, 128), F32),
            pltpu.VMEM((TAPS, 128, LANES), BF),
            pltpu.VMEM((PAD + LANES, 128), F32),
            pltpu.VMEM((LANES, 128), BF),
            pltpu.VMEM(share, F32),
            pltpu.VMEM(share, F32),
            pltpu.VMEM(share, BF),
            pltpu.VMEM(share, BF),
            pltpu.VMEM((ROWS, 128), F32),
            pltpu.VMEM((16, ROWS, 128), BF),
            pltpu.VMEM(share, BF),
            pltpu.VMEM(share, BF),
            pltpu.VMEM(share, BF),
            pltpu.VMEM(share, BF),
            dma((6,)), dma((TAPS,)),
            dma((34,)), dma((16,)), dma((16,)),
            dma((16,)), dma((16,)), dma((16,)), dma((16,)),
            dma((32,)), dma((32,)), dma((16,)), dma((16,)), dma((16,)), dma((16,)),
        ],
        compiler_params=pltpu.CompilerParams(
            collective_id=0, has_side_effects=True, vmem_limit_bytes=56 * 1024 * 1024
        ),
        name="gauss_newton",
    )(
        activations.T, act_tangent.T, kernel, kernel_tangent, slope, curvature,
        jnp.asarray(row_masks()), jnp.asarray(lane_masks()),
    )
    return pl.pallas_call(
        settle,
        out_shape=shapes,
        in_specs=[hbm, hbm],
        out_specs=(hbm, hbm),
        scratch_shapes=[
            pltpu.VMEM((SHARE, 128), BF), pltpu.VMEM((TAPS, 128, 128), F32), dma((4,)), dma((4,))
        ],
        name="settle",
    )(*results)


def solution(mesh):
    return jax.shard_map(
        per_device,
        mesh=mesh,
        in_specs=(
            P(None, ("chan", "filt")),
            P(None, ("chan", "filt")),
            P(None, "chan", "filt"),
            P(None, "chan", "filt"),
            P("chan", "filt"),
            P("chan", "filt"),
        ),
        out_specs=(P("filt", "chan"), P(None, "chan", "filt")),
        check_vma=False,
    )
```

```python
import jax
import jax.numpy as jnp
import numpy as np
from jax import lax
from jax.experimental import pallas as pl
from jax.experimental.pallas import tpu as pltpu
from jax.sharding import PartitionSpec as P

HH = 12
WW = 12
IMAGE = HH * WW
PIXELS = 2592
LANES = 2688
CUT = 1152
SHARE = 162
ROWS = 176
PARTS = ((0, 96), (96, 80))
PAD = 16
BLOCK = 384
TAPS = 9
BF = jnp.bfloat16
F32 = jnp.float32


def row_masks():
    r = np.arange(IMAGE + ROWS)
    i, j = (r // WW) % HH, r % WW
    m = np.stack([i >= 1, i <= HH - 2, j >= 1, j <= WW - 2]).astype(np.float32)
    return np.ascontiguousarray(np.broadcast_to(m[:, :, None], (*m.shape, 128)))


def lane_masks():
    p = np.arange(LANES)
    i, j = (p // WW) % HH, p % WW
    m = np.zeros((16, LANES), np.float32)
    for a in range(3):
        for e in range(3):
            si, sj = i + a - 1, j + e - 1
            m[3 * a + e] = (si >= 0) & (si < HH) & (sj >= 0) & (sj < WW) & (p < PIXELS)
    return m


def body(
    acts_ref, tans_ref, w_hbm, v_hbm, slope_hbm, curv_hbm, rmask_hbm, lmask_hbm,
    cot_ref, kp_hbm,
    w_ref, v_ref, slope_ref, curv_ref, rmask, lmask, kp_ref,
    gath, wcat, taps, xts, w32, w16, sib_out, sib_in, red_out, red_in, own,
    wgt, cx_out, cx_in, cz_out, cz_in,
    l_s, k_s,
    send_s, lo_rs, hi_rs, far_rs, s_rs, b_rs, w_rs, p_rs, x_rs, d_rs,
):
    chan = lax.axis_index("chan")
    filt = lax.axis_index("filt")
    core = lax.rem(chan, 2)
    chip = lax.div(chan, 2)
    half = lax.div(filt, 8)
    z = lax.rem(filt, 8)
    other = 1 - core
    sibling = {"chan": 2 * chip + other, "filt": filt}
    across = {"chan": chan, "filt": (1 - half) * 8 + z}

    def at_z(d):
        return lax.rem(z + d + 8, 8)

    def z_dev(d):
        return {"chan": chan, "filt": half * 8 + at_z(d)}

    def diag_dev(d):
        return {"chan": chan, "filt": (1 - half) * 8 + at_z(d)}

    def chip_at(j, sign=1):
        row = lax.rem(lax.div(chip, 2) + sign * lax.div(j, 2) + 4, 4)
        return 2 * row + lax.rem(chip + j, 2)

    def chip_dev(j):
        return {"chan": 2 * chip_at(j) + core, "filt": filt}

    def turns(i, middle):
        return middle + (1 - 2 * lax.rem(i, 2)) * lax.div(i + 1, 2)

    def chip_turn(i):
        return 2 * turns(lax.rem(i, 4), 2) + 1 - lax.div(i, 4)

    def z_turn(i):
        return turns(i, 4)

    def remote(src, dst, ss, rs, dev):
        return pltpu.make_async_remote_copy(
            src_ref=src, dst_ref=dst, send_sem=ss, recv_sem=rs,
            device_id=dev, device_id_type=pl.DeviceIdType.MESH,
        )

    barrier = pltpu.get_barrier_semaphore()
    peers = [sibling, across, diag_dev(1), diag_dev(-1)]
    peers += [z_dev(d) for d in range(1, 8)] + [chip_dev(jnp.int32(d)) for d in range(1, 8)]
    for dev in peers:
        pl.semaphore_signal(barrier, inc=1, device_id=dev, device_id_type=pl.DeviceIdType.MESH)

    pairs = [
        (v_hbm, v_ref), (w_hbm, w_ref), (rmask_hbm, rmask),
        (slope_hbm, slope_ref), (curv_hbm, curv_ref), (lmask_hbm, lmask),
    ]
    loads = [pltpu.make_async_copy(src, dst, l_s.at[n]) for n, (src, dst) in enumerate(pairs)]
    for c in loads:
        c.start()

    both = jnp.concatenate([acts_ref[...].astype(F32), tans_ref[...].astype(F32)], axis=0)
    both = jnp.concatenate([both, jnp.zeros((16, LANES - PIXELS), F32)], axis=1)
    gath[filt] = both.astype(BF)
    pl.semaphore_wait(barrier, len(peers))

    mine = half * 8
    theirs = (1 - half) * 8
    right, left = z_dev(1), z_dev(-1)
    LOW, HIGH = pl.ds(0, CUT), pl.ds(CUT, LANES - CUT)

    def piece(slot, lanes, sem, dev):
        ref = gath.at[slot, :, lanes]
        return remote(ref, ref, send_s.at[0], sem, dev)

    def send(slot, lanes, *devs, cross=False):
        for dev in devs:
            if cross:
                sem = far_rs.at[0]
            else:
                sem = lo_rs.at[slot] if lanes is LOW else hi_rs.at[lax.rem(slot, 8)]
            piece(slot, lanes, sem, dev).start()

    def got(slot, lanes):
        sem = lo_rs.at[slot] if lanes is LOW else hi_rs.at[lax.rem(slot, 8)]
        piece(slot, lanes, sem, across).wait_recv()

    send(filt, LOW, diag_dev(1), diag_dev(-1))
    send(filt, HIGH, right, left)
    send(filt, LOW, right, left, across)
    send(filt, HIGH, across, cross=True)

    for c in loads:
        c.wait()
    for k in range(TAPS):
        vk = v_ref[k].astype(F32).reshape(16, 1, 8, 128)
        wk = w_ref[k].astype(F32).reshape(16, 1, 8, 128)
        wcat[:, 128 * k:128 * k + 128] = (
            jnp.concatenate([vk, wk], axis=1).reshape(256, 128).astype(BF)
        )
        taps[k, 0:PAD, :] = jnp.zeros((PAD, 128), F32)

    for h in range(1, 5):
        slot = mine + at_z(-h)
        got(slot, HIGH)
        if h < 4:
            send(slot, HIGH, right)
            if h == 3:
                send(slot, HIGH, diag_dev(1), cross=True)
            send(slot, HIGH, across, cross=True)
            slot = mine + at_z(h)
            got(slot, HIGH)
            if h < 3:
                send(slot, HIGH, left)
            send(slot, HIGH, across, cross=True)
        for group in (mine, theirs):
            slot = group + at_z(h)
            got(slot, LOW)
            if h < 4:
                send(slot, LOW, left)
                slot = group + at_z(-h)
                got(slot, LOW)
                if h < 3:
                    send(slot, LOW, right)

    got(theirs + z, LOW)

    def forward(t, _):
        lanes = pl.ds(pl.multiple_of(t * BLOCK, 128), BLOCK)
        rows = pl.ds(pl.multiple_of(PAD + t * BLOCK, 16), BLOCK)
        x = gath[:, :, lanes].reshape(256, BLOCK).T
        for k in range(0, TAPS, 2):
            width = min(2, TAPS - k)
            res = jnp.dot(x, wcat[:, 128 * k:128 * (k + width)], preferred_element_type=F32)
            for q in range(width):
                taps[k + q, rows, :] = res[:, 128 * q:128 * q + 128]
        return 0

    lax.fori_loop(0, CUT // BLOCK, forward, 0, unroll=True)
    cross = gath.at[pl.ds(theirs, 8), :, HIGH]
    remote(cross, cross, send_s.at[0], far_rs.at[0], across).wait_recv()
    lax.fori_loop(CUT // BLOCK, LANES // BLOCK, forward, 0, unroll=True)

    def combined(c, flip, part, put):
        start = c * SHARE
        within = lax.rem(start, IMAGE)
        first, count = PARTS[part]
        step = count // 2
        for s in range(first, first + count, step):
            m = [rmask[n, pl.ds(within + s, step), :] for n in range(4)]
            acc = None
            for a in range(3):
                row = None
                for e in range(3):
                    k = 3 * a + e
                    off = WW * (a - 1) + e - 1
                    val = taps[8 - k if flip else k, pl.ds(PAD + start + s + off, step), :]
                    if e == 0:
                        val = val * m[2]
                    if e == 2:
                        val = val * m[3]
                    row = val if row is None else row + val
                if a == 0:
                    row = row * m[0]
                if a == 2:
                    row = row * m[1]
                acc = row if acc is None else acc + row
            put(s, step, acc)

    def rows_of(part):
        return pl.ds(*PARTS[part])

    def sib_copy(d, part):
        return remote(
            sib_out.at[d, rows_of(part)], sib_in.at[d, rows_of(part)],
            send_s.at[1], s_rs.at[2 * d + part], sibling,
        )

    def to_sibling(i, part):
        d = chip_at(chip_turn(i))

        def put(s, n, acc):
            sib_out[d, s:s + n, :] = acc

        combined(2 * d + other, False, part, put)
        sib_copy(d, part).start()

    def red_copy(j, part):
        return remote(
            red_out.at[j, rows_of(part)], red_in.at[j, rows_of(part)],
            send_s.at[2], b_rs.at[part], chip_dev(j),
        )

    def to_chip(i, part):
        j = chip_turn(i)
        d = chip_at(j)
        sib_copy(d, part).wait_recv()

        def put(s, n, acc):
            red_out[j, s:s + n, :] = (acc + sib_in[d, s:s + n, :]).astype(BF)

        combined(2 * d + core, False, part, put)
        red_copy(j, part).start()

    def ahead(first, last, part, step=None, chip_part=None):
        def go(i, _):
            to_sibling(i, part)
            if step is not None:
                to_chip(i + step, chip_part)
            return 0

        lax.fori_loop(first, last, go, 0)

    def behind(i, _):
        to_chip(i, 1)
        return 0

    ahead(0, 4, 0)
    ahead(4, 8, 0, -4, 0)
    ahead(0, 3, 1, 4, 0)
    ahead(3, 4, 1)
    ahead(4, 8, 1, -4, 1)
    lax.fori_loop(4, 7, behind, 0)

    def put_own(s, n, acc):
        own[s:s + n, :] = acc + sib_in[chip, s:s + n, :]

    for part in range(2):
        sib_copy(chip, part).wait_recv()
        combined(2 * chip + core, False, part, put_own)

    def shift(t, _):
        g = gath[pl.ds(2 * t, 2)].astype(F32)
        x = g[:, 0:8, :].reshape(16, LANES)
        rows = pl.ds(pl.multiple_of(16 * t, 16), 16)
        for e in range(3):
            xe = x if e == 1 else pltpu.roll(x, (1 - e) % LANES, 1)
            for a in range(3):
                k = 3 * a + e
                xk = xe if a == 1 else pltpu.roll(xe, (WW * (1 - a)) % LANES, 1)
                xts[k, rows, :] = (xk * lmask[k:k + 1, :]).astype(BF)
        return 0

    lax.fori_loop(0, 4, shift, 0)

    def wgt_copy(slot, part, dev):
        ref = wgt.at[slot, rows_of(part)]
        return remote(ref, ref, send_s.at[3], w_rs.at[2 * lax.div(slot, 2) + part], dev)

    def sib_wgt_copy(slot, part):
        ref = wgt.at[slot, rows_of(part)]
        return remote(ref, ref, send_s.at[3], p_rs.at[part], sibling)

    for part, (first, count) in enumerate(PARTS):
        rows = slice(first, first + count)

        all_in = red_in.at[pl.ds(1, 7), rows_of(part)]
        remote(all_in, all_in, send_s.at[2], b_rs.at[part], sibling).wait_recv()
        total = own[rows, :]
        for j in range(1, 8):
            total = total + red_in[j, rows, :].astype(F32)
        valid = min(first + count, SHARE) - first
        slope = slope_ref[first:first + valid, :].astype(F32)
        curv = curv_ref[first:first + valid, :].astype(F32)
        weighted = slope * slope * curv * total[:valid]
        if valid < count:
            weighted = jnp.concatenate([weighted, jnp.zeros((count - valid, 128), F32)], axis=0)
        wgt[chan, rows, :] = weighted.astype(BF)

        def spread(i, _, part=part):
            j = chip_turn(i)
            wgt_copy(chan, part, chip_dev(j)).start()
            return 0

        lax.fori_loop(0, 7, spread, 0)
        sib_wgt_copy(chan, part).start()

    lax.fori_loop(4, 8, shift, 0)

    def unpack(c, part):
        start = c * SHARE
        first, count = PARTS[part]
        x = wgt[c, rows_of(part), :].astype(F32)
        if part == 0:
            w32[pl.ds(start, 96), :] = x
        else:
            w32[pl.ds(start + 96, 64), :] = x[0:64]
            w32[pl.ds(start + 160, 2), :] = x[64:66]

    for part in range(2):

        def pass_on(i, _, part=part):
            j = chip_turn(i)
            slot = 2 * chip_at(j, -1) + core
            wgt_copy(slot, part, sibling).wait_recv()
            sib_wgt_copy(slot, part).start()
            unpack(slot, part)
            return 0

        unpack(chan, part)
        lax.fori_loop(0, 7, pass_on, 0)

    for part in range(2):

        def from_sibling(i, _, part=part):
            unpack(2 * i + other, part)
            return 0

        passed = wgt.at[pl.ds(0, 8), rows_of(part)]
        remote(passed, passed, send_s.at[3], p_rs.at[part], sibling).wait_recv()

        lax.fori_loop(0, 8, from_sibling, 0)
    w32[PIXELS:LANES, :] = jnp.zeros((LANES - PIXELS, 128), F32)

    def backward(i, _):
        t = lax.rem(i + 3 * (1 - half), LANES // BLOCK)
        rows = pl.ds(pl.multiple_of(t * BLOCK, 16), BLOCK)
        spot = pl.ds(pl.multiple_of(PAD + t * BLOCK, 16), BLOCK)
        w = w32[rows, :].astype(BF)
        w16[rows, :] = w
        for k in range(0, TAPS, 2):
            width = min(2, TAPS - k)
            kern = w_ref[k:k + width].reshape(128 * width, 128)
            res = lax.dot_general(w, kern, (((1,), (1,)), ((), ())), preferred_element_type=F32)
            for q in range(width):
                taps[k + q, spot, :] = res[:, 128 * q:128 * q + 128]
        return 0

    lax.fori_loop(0, 4, backward, 0, unroll=True)

    scale = F32(1.0) / jnp.sqrt(F32(PIXELS))

    def kp_copy(k):
        return pltpu.make_async_copy(kp_ref.at[k], kp_hbm.at[k], k_s.at[0])

    def product(k):
        kp_ref[k] = jnp.dot(xts[k], w16[...], preferred_element_type=F32) * scale
        kp_copy(k).start()

    def cx_copy(j, part):
        return remote(
            cx_out.at[j, rows_of(part)], cx_in.at[j, rows_of(part)],
            send_s.at[4], x_rs.at[2 * j + part], across,
        )

    def cz_copy(j, part):
        return remote(
            cz_out.at[j, rows_of(part)], cz_in.at[j, rows_of(part)],
            send_s.at[5], d_rs.at[0], z_dev(j),
        )

    def to_across(i, _):
        j = z_turn(i)

        def put(s, n, acc):
            cx_out[j, s:s + n, :] = acc.astype(BF)

        for part in range(2):
            combined(theirs + at_z(j), True, part, put)
            cx_copy(j, part).start()
        return 0

    lax.fori_loop(0, 8, to_across, 0)
    lax.fori_loop(4, LANES // BLOCK, backward, 0, unroll=True)

    def to_z(i, _):
        j = z_turn(i)

        def put(s, n, acc):
            cz_out[j, s:s + n, :] = (acc + cx_in[j, s:s + n, :].astype(F32)).astype(BF)

        for part in range(2):
            cx_copy(j, part).wait_recv()
            combined(mine + at_z(j), True, part, put)
            cz_copy(j, part).start()
        product(i)
        return 0

    lax.fori_loop(0, 7, to_z, 0)

    def put_last(s, n, acc):
        own[s:s + n, :] = acc + cx_in[0, s:s + n, :].astype(F32)

    for part in range(2):
        cx_copy(0, part).wait_recv()
        combined(mine + z, True, part, put_last)
    product(7)
    product(8)

    others = pl.ds(1, 7)
    remote(cz_in.at[others], cz_in.at[others], send_s.at[5], d_rs.at[0], across).wait_recv()
    total = own[...]
    for j in range(1, 8):
        total = total + cz_in[j].astype(F32)
    cot_ref[...] = total[0:SHARE].astype(BF)

    pltpu.make_async_copy(kp_ref, kp_hbm, k_s.at[0]).wait()
    spent = [
        gath.at[pl.ds(0, 15)], sib_out, red_out.at[others],
        wgt.at[pl.ds(0, 15)], cx_out, cz_out.at[others],
    ]
    for n, ref in enumerate(spent):
        remote(ref, ref, send_s.at[n], d_rs.at[0], across).wait_send()


def settle(cot_in, kp_in, cot_ref, kp_ref, cot_v, kp_v, in_s, out_s):
    legs = [(cot_in, cot_v, cot_ref)]
    for n in range(3):
        part = pl.ds(3 * n, 3)
        legs.append((kp_in.at[part], kp_v.at[part], kp_ref.at[part]))
    for n, (src, via, _) in enumerate(legs):
        pltpu.make_async_copy(src, via, in_s.at[n]).start()
    for n, (src, via, dst) in enumerate(legs):
        pltpu.make_async_copy(src, via, in_s.at[n]).wait()
        pltpu.make_async_copy(via, dst, out_s.at[n]).start()
    for n, (_, via, dst) in enumerate(legs):
        pltpu.make_async_copy(via, dst, out_s.at[n]).wait()


def per_device(activations, act_tangent, kernel, kernel_tangent, slope, curvature):
    vm = pl.BlockSpec(memory_space=pltpu.VMEM)
    hbm = pl.BlockSpec(memory_space=pl.ANY)
    dma = pltpu.SemaphoreType.DMA
    share = (8, ROWS, 128)
    shapes = (
        jax.ShapeDtypeStruct((SHARE, 128), BF),
        jax.ShapeDtypeStruct((TAPS, 128, 128), F32),
    )
    results = pl.pallas_call(
        body,
        out_shape=shapes,
        in_specs=[vm] * 2 + [hbm] * 6,
        out_specs=(vm, hbm),
        scratch_shapes=[
            pltpu.VMEM((TAPS, 128, 128), BF),
            pltpu.VMEM((TAPS, 128, 128), BF),
            pltpu.VMEM((SHARE, 128), BF),
            pltpu.VMEM((SHARE, 128), BF),
            pltpu.VMEM((4, IMAGE + ROWS, 128), F32),
            pltpu.VMEM((16, LANES), F32),
            pltpu.VMEM((TAPS, 128, 128), F32),
            pltpu.VMEM((16, 16, LANES), BF),
            pltpu.VMEM((256, TAPS * 128), BF),
            pltpu.VMEM((TAPS, PAD + LANES, 128), F32),
            pltpu.VMEM((TAPS, 128, LANES), BF),
            pltpu.VMEM((PAD + LANES, 128), F32),
            pltpu.VMEM((LANES, 128), BF),
            pltpu.VMEM(share, F32),
            pltpu.VMEM(share, F32),
            pltpu.VMEM(share, BF),
            pltpu.VMEM(share, BF),
            pltpu.VMEM((ROWS, 128), F32),
            pltpu.VMEM((16, ROWS, 128), BF),
            pltpu.VMEM(share, BF),
            pltpu.VMEM(share, BF),
            pltpu.VMEM(share, BF),
            pltpu.VMEM(share, BF),
            dma((6,)), dma((1,)), dma((6,)),
            dma((16,)), dma((8,)), dma((1,)), dma((16,)), dma((2,)),
            dma((16,)), dma((2,)), dma((16,)), dma((1,)),
        ],
        compiler_params=pltpu.CompilerParams(
            collective_id=0, has_side_effects=True, vmem_limit_bytes=56 * 1024 * 1024
        ),
        name="gauss_newton",
    )(
        activations.T, act_tangent.T, kernel, kernel_tangent, slope, curvature,
        jnp.asarray(row_masks()), jnp.asarray(lane_masks()),
    )
    return pl.pallas_call(
        settle,
        out_shape=shapes,
        in_specs=[hbm, hbm],
        out_specs=(hbm, hbm),
        scratch_shapes=[
            pltpu.VMEM((SHARE, 128), BF), pltpu.VMEM((TAPS, 128, 128), F32), dma((4,)), dma((4,))
        ],
        name="settle",
    )(*results)


def solution(mesh):
    return jax.shard_map(
        per_device,
        mesh=mesh,
        in_specs=(
            P(None, ("chan", "filt")),
            P(None, ("chan", "filt")),
            P(None, "chan", "filt"),
            P(None, "chan", "filt"),
            P("chan", "filt"),
            P("chan", "filt"),
        ),
        out_specs=(P("filt", "chan"), P(None, "chan", "filt")),
        check_vma=False,
    )
```

```python
import jax
import jax.numpy as jnp
import numpy as np
from jax import lax
from jax.experimental import pallas as pl
from jax.experimental.pallas import tpu as pltpu
from jax.sharding import PartitionSpec as P

HH = 12
WW = 12
IMAGE = HH * WW
PIXELS = 2592
LANES = 2688
CUT = 1152
SHARE = 162
ROWS = 176
PARTS = ((0, 96), (96, 80))
PAD = 16
BLOCK = 384
TAPS = 9
BF = jnp.bfloat16
F32 = jnp.float32


def row_masks():
    r = np.arange(IMAGE + ROWS)
    i, j = (r // WW) % HH, r % WW
    m = np.stack([i >= 1, i <= HH - 2, j >= 1, j <= WW - 2]).astype(np.float32)
    return np.ascontiguousarray(np.broadcast_to(m[:, :, None], (*m.shape, 128)))


def lane_masks():
    p = np.arange(LANES)
    i, j = (p // WW) % HH, p % WW
    m = np.zeros((16, LANES), np.float32)
    for a in range(3):
        for e in range(3):
            si, sj = i + a - 1, j + e - 1
            m[3 * a + e] = (si >= 0) & (si < HH) & (sj >= 0) & (sj < WW) & (p < PIXELS)
    return m


def body(
    acts_hbm, tans_hbm, w_hbm, v_hbm, slope_hbm, curv_hbm, rmask_hbm, lmask_hbm,
    cot_ref, kp_hbm,
    acts_ref, tans_ref, w_ref, v_ref, slope_ref, curv_ref, rmask, lmask, kp_ref,
    gath, wcat, taps, xts, w32, w16, sib_out, sib_in, red_out, red_in, own,
    wgt, cx_out, cx_in, cz_out, cz_in,
    l_s, k_s,
    send_s, lo_rs, hi_rs, far_rs, s_rs, b_rs, w_rs, p_rs, x_rs, d_rs,
):
    chan = lax.axis_index("chan")
    filt = lax.axis_index("filt")
    core = lax.rem(chan, 2)
    chip = lax.div(chan, 2)
    half = lax.div(filt, 8)
    z = lax.rem(filt, 8)
    other = 1 - core
    sibling = {"chan": 2 * chip + other, "filt": filt}
    across = {"chan": chan, "filt": (1 - half) * 8 + z}

    def at_z(d):
        return lax.rem(z + d + 8, 8)

    def z_dev(d):
        return {"chan": chan, "filt": half * 8 + at_z(d)}

    def diag_dev(d):
        return {"chan": chan, "filt": (1 - half) * 8 + at_z(d)}

    def chip_at(j, sign=1):
        row = lax.rem(lax.div(chip, 2) + sign * lax.div(j, 2) + 4, 4)
        return 2 * row + lax.rem(chip + j, 2)

    def chip_dev(j):
        return {"chan": 2 * chip_at(j) + core, "filt": filt}

    def turns(i, middle):
        return middle + (1 - 2 * lax.rem(i, 2)) * lax.div(i + 1, 2)

    def chip_turn(i):
        return 2 * turns(lax.rem(i, 4), 2) + 1 - lax.div(i, 4)

    def z_turn(i):
        return turns(i, 4)

    def remote(src, dst, ss, rs, dev):
        return pltpu.make_async_remote_copy(
            src_ref=src, dst_ref=dst, send_sem=ss, recv_sem=rs,
            device_id=dev, device_id_type=pl.DeviceIdType.MESH,
        )

    barrier = pltpu.get_barrier_semaphore()
    peers = [sibling, across, diag_dev(1), diag_dev(-1)]
    peers += [z_dev(d) for d in range(1, 8)] + [chip_dev(jnp.int32(d)) for d in range(1, 8)]
    for dev in peers:
        pl.semaphore_signal(barrier, inc=1, device_id=dev, device_id_type=pl.DeviceIdType.MESH)

    pairs = [
        (acts_hbm, acts_ref), (tans_hbm, tans_ref), (v_hbm, v_ref), (w_hbm, w_ref), (rmask_hbm, rmask),
        (slope_hbm, slope_ref), (curv_hbm, curv_ref), (lmask_hbm, lmask),
    ]
    loads = [pltpu.make_async_copy(src, dst, l_s.at[n]) for n, (src, dst) in enumerate(pairs)]
    for c in loads:
        c.start()
    for c in loads[:2]:
        c.wait()

    both = jnp.concatenate([acts_ref[...].astype(F32), tans_ref[...].astype(F32)], axis=0)
    both = jnp.concatenate([both, jnp.zeros((16, LANES - PIXELS), F32)], axis=1)
    gath[filt] = both.astype(BF)
    pl.semaphore_wait(barrier, len(peers))

    mine = half * 8
    theirs = (1 - half) * 8
    right, left = z_dev(1), z_dev(-1)
    LOW, HIGH = pl.ds(0, CUT), pl.ds(CUT, LANES - CUT)

    def piece(slot, lanes, sem, dev):
        ref = gath.at[slot, :, lanes]
        return remote(ref, ref, send_s.at[0], sem, dev)

    def send(slot, lanes, *devs, cross=False):
        for dev in devs:
            if cross:
                sem = far_rs.at[0]
            else:
                sem = lo_rs.at[slot] if lanes is LOW else hi_rs.at[lax.rem(slot, 8)]
            piece(slot, lanes, sem, dev).start()

    def got(slot, lanes):
        sem = lo_rs.at[slot] if lanes is LOW else hi_rs.at[lax.rem(slot, 8)]
        piece(slot, lanes, sem, across).wait_recv()

    send(filt, LOW, diag_dev(1), diag_dev(-1))
    send(filt, HIGH, right, left)
    send(filt, LOW, right, left, across)
    send(filt, HIGH, across, cross=True)

    for c in loads[2:]:
        c.wait()
    for k in range(TAPS):
        vk = v_ref[k].astype(F32).reshape(16, 1, 8, 128)
        wk = w_ref[k].astype(F32).reshape(16, 1, 8, 128)
        wcat[:, 128 * k:128 * k + 128] = (
            jnp.concatenate([vk, wk], axis=1).reshape(256, 128).astype(BF)
        )
        taps[k, 0:PAD, :] = jnp.zeros((PAD, 128), F32)

    for h in range(1, 5):
        slot = mine + at_z(-h)
        got(slot, HIGH)
        if h < 4:
            send(slot, HIGH, right)
            if h == 3:
                send(slot, HIGH, diag_dev(1), cross=True)
            send(slot, HIGH, across, cross=True)
            slot = mine + at_z(h)
            got(slot, HIGH)
            if h < 3:
                send(slot, HIGH, left)
            send(slot, HIGH, across, cross=True)
        for group in (mine, theirs):
            slot = group + at_z(h)
            got(slot, LOW)
            if h < 4:
                send(slot, LOW, left)
                slot = group + at_z(-h)
                got(slot, LOW)
                if h < 3:
                    send(slot, LOW, right)

    got(theirs + z, LOW)

    def forward(t, _):
        lanes = pl.ds(pl.multiple_of(t * BLOCK, 128), BLOCK)
        rows = pl.ds(pl.multiple_of(PAD + t * BLOCK, 16), BLOCK)
        x = gath[:, :, lanes].reshape(256, BLOCK).T
        for k in range(0, TAPS, 2):
            width = min(2, TAPS - k)
            res = jnp.dot(x, wcat[:, 128 * k:128 * (k + width)], preferred_element_type=F32)
            for q in range(width):
                taps[k + q, rows, :] = res[:, 128 * q:128 * q + 128]
        return 0

    lax.fori_loop(0, CUT // BLOCK, forward, 0, unroll=True)
    cross = gath.at[pl.ds(theirs, 8), :, HIGH]
    remote(cross, cross, send_s.at[0], far_rs.at[0], across).wait_recv()
    lax.fori_loop(CUT // BLOCK, LANES // BLOCK, forward, 0, unroll=True)

    def combined(c, flip, part, put):
        start = c * SHARE
        within = lax.rem(start, IMAGE)
        first, count = PARTS[part]
        step = count // 2
        for s in range(first, first + count, step):
            m = [rmask[n, pl.ds(within + s, step), :] for n in range(4)]
            acc = None
            for a in range(3):
                row = None
                for e in range(3):
                    k = 3 * a + e
                    off = WW * (a - 1) + e - 1
                    val = taps[8 - k if flip else k, pl.ds(PAD + start + s + off, step), :]
                    if e == 0:
                        val = val * m[2]
                    if e == 2:
                        val = val * m[3]
                    row = val if row is None else row + val
                if a == 0:
                    row = row * m[0]
                if a == 2:
                    row = row * m[1]
                acc = row if acc is None else acc + row
            put(s, step, acc)

    def rows_of(part):
        return pl.ds(*PARTS[part])

    def sib_copy(d, part):
        return remote(
            sib_out.at[d, rows_of(part)], sib_in.at[d, rows_of(part)],
            send_s.at[1], s_rs.at[2 * d + part], sibling,
        )

    def to_sibling(i, part):
        d = chip_at(chip_turn(i))

        def put(s, n, acc):
            sib_out[d, s:s + n, :] = acc

        combined(2 * d + other, False, part, put)
        sib_copy(d, part).start()

    def red_copy(j, part):
        return remote(
            red_out.at[j, rows_of(part)], red_in.at[j, rows_of(part)],
            send_s.at[2], b_rs.at[part], chip_dev(j),
        )

    def to_chip(i, part):
        j = chip_turn(i)
        d = chip_at(j)
        sib_copy(d, part).wait_recv()

        def put(s, n, acc):
            red_out[j, s:s + n, :] = (acc + sib_in[d, s:s + n, :]).astype(BF)

        combined(2 * d + core, False, part, put)
        red_copy(j, part).start()

    def ahead(first, last, part, step=None, chip_part=None):
        def go(i, _):
            to_sibling(i, part)
            if step is not None:
                to_chip(i + step, chip_part)
            return 0

        lax.fori_loop(first, last, go, 0)

    def behind(i, _):
        to_chip(i, 1)
        return 0

    ahead(0, 4, 0)
    ahead(4, 8, 0, -4, 0)
    ahead(0, 3, 1, 4, 0)
    ahead(3, 4, 1)
    ahead(4, 8, 1, -4, 1)
    lax.fori_loop(4, 7, behind, 0)

    def put_own(s, n, acc):
        own[s:s + n, :] = acc + sib_in[chip, s:s + n, :]

    for part in range(2):
        sib_copy(chip, part).wait_recv()
        combined(2 * chip + core, False, part, put_own)

    def shift(t, _):
        g = gath[pl.ds(2 * t, 2)].astype(F32)
        x = g[:, 0:8, :].reshape(16, LANES)
        rows = pl.ds(pl.multiple_of(16 * t, 16), 16)
        for e in range(3):
            xe = x if e == 1 else pltpu.roll(x, (1 - e) % LANES, 1)
            for a in range(3):
                k = 3 * a + e
                xk = xe if a == 1 else pltpu.roll(xe, (WW * (1 - a)) % LANES, 1)
                xts[k, rows, :] = (xk * lmask[k:k + 1, :]).astype(BF)
        return 0

    lax.fori_loop(0, 4, shift, 0)

    def wgt_copy(slot, part, dev):
        ref = wgt.at[slot, rows_of(part)]
        return remote(ref, ref, send_s.at[3], w_rs.at[2 * lax.div(slot, 2) + part], dev)

    def sib_wgt_copy(slot, part):
        ref = wgt.at[slot, rows_of(part)]
        return remote(ref, ref, send_s.at[3], p_rs.at[part], sibling)

    for part, (first, count) in enumerate(PARTS):
        rows = slice(first, first + count)

        all_in = red_in.at[pl.ds(1, 7), rows_of(part)]
        remote(all_in, all_in, send_s.at[2], b_rs.at[part], sibling).wait_recv()
        total = own[rows, :]
        for j in range(1, 8):
            total = total + red_in[j, rows, :].astype(F32)
        valid = min(first + count, SHARE) - first
        slope = slope_ref[first:first + valid, :].astype(F32)
        curv = curv_ref[first:first + valid, :].astype(F32)
        weighted = slope * slope * curv * total[:valid]
        if valid < count:
            weighted = jnp.concatenate([weighted, jnp.zeros((count - valid, 128), F32)], axis=0)
        wgt[chan, rows, :] = weighted.astype(BF)

        def spread(i, _, part=part):
            j = chip_turn(i)
            wgt_copy(chan, part, chip_dev(j)).start()
            return 0

        lax.fori_loop(0, 7, spread, 0)
        sib_wgt_copy(chan, part).start()

    lax.fori_loop(4, 8, shift, 0)

    def unpack(c, part):
        start = c * SHARE
        first, count = PARTS[part]
        x = wgt[c, rows_of(part), :].astype(F32)
        if part == 0:
            w32[pl.ds(start, 96), :] = x
        else:
            w32[pl.ds(start + 96, 64), :] = x[0:64]
            w32[pl.ds(start + 160, 2), :] = x[64:66]

    for part in range(2):

        def pass_on(i, _, part=part):
            j = chip_turn(i)
            slot = 2 * chip_at(j, -1) + core
            wgt_copy(slot, part, sibling).wait_recv()
            sib_wgt_copy(slot, part).start()
            unpack(slot, part)
            return 0

        unpack(chan, part)
        lax.fori_loop(0, 7, pass_on, 0)

    for part in range(2):

        def from_sibling(i, _, part=part):
            unpack(2 * i + other, part)
            return 0

        passed = wgt.at[pl.ds(0, 8), rows_of(part)]
        remote(passed, passed, send_s.at[3], p_rs.at[part], sibling).wait_recv()

        lax.fori_loop(0, 8, from_sibling, 0)
    w32[PIXELS:LANES, :] = jnp.zeros((LANES - PIXELS, 128), F32)

    def backward(i, _):
        t = lax.rem(i + 3 * (1 - half), LANES // BLOCK)
        rows = pl.ds(pl.multiple_of(t * BLOCK, 16), BLOCK)
        spot = pl.ds(pl.multiple_of(PAD + t * BLOCK, 16), BLOCK)
        w = w32[rows, :].astype(BF)
        w16[rows, :] = w
        for k in range(0, TAPS, 2):
            width = min(2, TAPS - k)
            kern = w_ref[k:k + width].reshape(128 * width, 128)
            res = lax.dot_general(w, kern, (((1,), (1,)), ((), ())), preferred_element_type=F32)
            for q in range(width):
                taps[k + q, spot, :] = res[:, 128 * q:128 * q + 128]
        return 0

    lax.fori_loop(0, 4, backward, 0, unroll=True)

    scale = F32(1.0) / jnp.sqrt(F32(PIXELS))

    def kp_copy(k):
        return pltpu.make_async_copy(kp_ref.at[k], kp_hbm.at[k], k_s.at[0])

    def product(k):
        kp_ref[k] = jnp.dot(xts[k], w16[...], preferred_element_type=F32) * scale
        kp_copy(k).start()

    def cx_copy(j, part):
        return remote(
            cx_out.at[j, rows_of(part)], cx_in.at[j, rows_of(part)],
            send_s.at[4], x_rs.at[2 * j + part], across,
        )

    def cz_copy(j, part):
        return remote(
            cz_out.at[j, rows_of(part)], cz_in.at[j, rows_of(part)],
            send_s.at[5], d_rs.at[0], z_dev(j),
        )

    def to_across(i, _):
        j = z_turn(i)

        def put(s, n, acc):
            cx_out[j, s:s + n, :] = acc.astype(BF)

        for part in range(2):
            combined(theirs + at_z(j), True, part, put)
            cx_copy(j, part).start()
        return 0

    lax.fori_loop(0, 8, to_across, 0)
    lax.fori_loop(4, LANES // BLOCK, backward, 0, unroll=True)

    def to_z(i, _):
        j = z_turn(i)

        def put(s, n, acc):
            cz_out[j, s:s + n, :] = (acc + cx_in[j, s:s + n, :].astype(F32)).astype(BF)

        for part in range(2):
            cx_copy(j, part).wait_recv()
            combined(mine + at_z(j), True, part, put)
            cz_copy(j, part).start()
        product(i)
        return 0

    lax.fori_loop(0, 7, to_z, 0)

    def put_last(s, n, acc):
        own[s:s + n, :] = acc + cx_in[0, s:s + n, :].astype(F32)

    for part in range(2):
        cx_copy(0, part).wait_recv()
        combined(mine + z, True, part, put_last)
    product(7)
    product(8)

    others = pl.ds(1, 7)
    remote(cz_in.at[others], cz_in.at[others], send_s.at[5], d_rs.at[0], across).wait_recv()
    total = own[...]
    for j in range(1, 8):
        total = total + cz_in[j].astype(F32)
    cot_ref[...] = total[0:SHARE].astype(BF)

    pltpu.make_async_copy(kp_ref, kp_hbm, k_s.at[0]).wait()
    spent = [
        gath.at[pl.ds(0, 15)], sib_out, red_out.at[others],
        wgt.at[pl.ds(0, 15)], cx_out, cz_out.at[others],
    ]
    for n, ref in enumerate(spent):
        remote(ref, ref, send_s.at[n], d_rs.at[0], across).wait_send()


def settle(cot_in, kp_in, cot_ref, kp_ref, cot_v, kp_v, in_s, out_s):
    legs = [(cot_in, cot_v, cot_ref)]
    for n in range(3):
        part = pl.ds(3 * n, 3)
        legs.append((kp_in.at[part], kp_v.at[part], kp_ref.at[part]))
    for n, (src, via, _) in enumerate(legs):
        pltpu.make_async_copy(src, via, in_s.at[n]).start()
    for n, (src, via, dst) in enumerate(legs):
        pltpu.make_async_copy(src, via, in_s.at[n]).wait()
        pltpu.make_async_copy(via, dst, out_s.at[n]).start()
    for n, (_, via, dst) in enumerate(legs):
        pltpu.make_async_copy(via, dst, out_s.at[n]).wait()


def per_device(activations, act_tangent, kernel, kernel_tangent, slope, curvature):
    vm = pl.BlockSpec(memory_space=pltpu.VMEM)
    hbm = pl.BlockSpec(memory_space=pl.ANY)
    dma = pltpu.SemaphoreType.DMA
    share = (8, ROWS, 128)
    shapes = (
        jax.ShapeDtypeStruct((SHARE, 128), BF),
        jax.ShapeDtypeStruct((TAPS, 128, 128), F32),
    )
    results = pl.pallas_call(
        body,
        out_shape=shapes,
        in_specs=[hbm] * 8,
        out_specs=(vm, hbm),
        scratch_shapes=[
            pltpu.VMEM((8, PIXELS), BF),
            pltpu.VMEM((8, PIXELS), BF),
            pltpu.VMEM((TAPS, 128, 128), BF),
            pltpu.VMEM((TAPS, 128, 128), BF),
            pltpu.VMEM((SHARE, 128), BF),
            pltpu.VMEM((SHARE, 128), BF),
            pltpu.VMEM((4, IMAGE + ROWS, 128), F32),
            pltpu.VMEM((16, LANES), F32),
            pltpu.VMEM((TAPS, 128, 128), F32),
            pltpu.VMEM((16, 16, LANES), BF),
            pltpu.VMEM((256, TAPS * 128), BF),
            pltpu.VMEM((TAPS, PAD + LANES, 128), F32),
            pltpu.VMEM((TAPS, 128, LANES), BF),
            pltpu.VMEM((PAD + LANES, 128), F32),
            pltpu.VMEM((LANES, 128), BF),
            pltpu.VMEM(share, F32),
            pltpu.VMEM(share, F32),
            pltpu.VMEM(share, BF),
            pltpu.VMEM(share, BF),
            pltpu.VMEM((ROWS, 128), F32),
            pltpu.VMEM((16, ROWS, 128), BF),
            pltpu.VMEM(share, BF),
            pltpu.VMEM(share, BF),
            pltpu.VMEM(share, BF),
            pltpu.VMEM(share, BF),
            dma((8,)), dma((1,)), dma((6,)),
            dma((16,)), dma((8,)), dma((1,)), dma((16,)), dma((2,)),
            dma((16,)), dma((2,)), dma((16,)), dma((1,)),
        ],
        compiler_params=pltpu.CompilerParams(
            collective_id=0, has_side_effects=True, vmem_limit_bytes=56 * 1024 * 1024
        ),
        name="gauss_newton",
    )(
        activations.T, act_tangent.T, kernel, kernel_tangent, slope, curvature,
        jnp.asarray(row_masks()), jnp.asarray(lane_masks()),
    )
    return pl.pallas_call(
        settle,
        out_shape=shapes,
        in_specs=[hbm, hbm],
        out_specs=(hbm, hbm),
        scratch_shapes=[
            pltpu.VMEM((SHARE, 128), BF), pltpu.VMEM((TAPS, 128, 128), F32), dma((4,)), dma((4,))
        ],
        name="settle",
    )(*results)


def solution(mesh):
    return jax.shard_map(
        per_device,
        mesh=mesh,
        in_specs=(
            P(None, ("chan", "filt")),
            P(None, ("chan", "filt")),
            P(None, "chan", "filt"),
            P(None, "chan", "filt"),
            P("chan", "filt"),
            P("chan", "filt"),
        ),
        out_specs=(P("filt", "chan"), P(None, "chan", "filt")),
        check_vma=False,
    )
```

```python
import jax
import jax.numpy as jnp
import numpy as np
from jax import lax
from jax.experimental import pallas as pl
from jax.experimental.pallas import tpu as pltpu
from jax.sharding import PartitionSpec as P

HH = 12
WW = 12
IMAGE = HH * WW
PIXELS = 2592
LANES = 2688
CUT = 1152
SHARE = 162
ROWS = 176
PARTS = ((0, 80), (80, 96))
PAD = 16
BLOCK = 384
TAPS = 9
BF = jnp.bfloat16
F32 = jnp.float32


def row_masks():
    r = np.arange(IMAGE + ROWS)
    i, j = (r // WW) % HH, r % WW
    m = np.stack([i >= 1, i <= HH - 2, j >= 1, j <= WW - 2]).astype(np.float32)
    return np.ascontiguousarray(np.broadcast_to(m[:, :, None], (*m.shape, 128)))


def lane_masks():
    p = np.arange(LANES)
    i, j = (p // WW) % HH, p % WW
    m = np.zeros((16, LANES), np.float32)
    for a in range(3):
        for e in range(3):
            si, sj = i + a - 1, j + e - 1
            m[3 * a + e] = (si >= 0) & (si < HH) & (sj >= 0) & (sj < WW) & (p < PIXELS)
    return m


def body(
    acts_hbm, tans_hbm, w_hbm, v_hbm, slope_hbm, curv_hbm, rmask_hbm, lmask_hbm,
    cot_ref, kp_hbm,
    acts_ref, tans_ref, w_ref, v_ref, slope_ref, curv_ref, rmask, lmask, kp_ref,
    gath, wcat, taps, xts, w32, w16, sib_out, sib_in, red_out, red_in, own,
    wgt, cx_out, cx_in, cz_out, cz_in,
    l_s, k_s,
    send_s, lo_rs, hi_rs, far_rs, s_rs, b_rs, w_rs, p_rs, x_rs, d_rs,
):
    chan = lax.axis_index("chan")
    filt = lax.axis_index("filt")
    core = lax.rem(chan, 2)
    chip = lax.div(chan, 2)
    half = lax.div(filt, 8)
    z = lax.rem(filt, 8)
    other = 1 - core
    sibling = {"chan": 2 * chip + other, "filt": filt}
    across = {"chan": chan, "filt": (1 - half) * 8 + z}

    def at_z(d):
        return lax.rem(z + d + 8, 8)

    def z_dev(d):
        return {"chan": chan, "filt": half * 8 + at_z(d)}

    def diag_dev(d):
        return {"chan": chan, "filt": (1 - half) * 8 + at_z(d)}

    def chip_at(j, sign=1):
        row = lax.rem(lax.div(chip, 2) + sign * lax.div(j, 2) + 4, 4)
        return 2 * row + lax.rem(chip + j, 2)

    def chip_dev(j):
        return {"chan": 2 * chip_at(j) + core, "filt": filt}

    def turns(i, middle):
        return middle + (1 - 2 * lax.rem(i, 2)) * lax.div(i + 1, 2)

    def chip_turn(i):
        return 2 * turns(lax.rem(i, 4), 2) + 1 - lax.div(i, 4)

    def z_turn(i):
        return turns(i, 4)

    def remote(src, dst, ss, rs, dev):
        return pltpu.make_async_remote_copy(
            src_ref=src, dst_ref=dst, send_sem=ss, recv_sem=rs,
            device_id=dev, device_id_type=pl.DeviceIdType.MESH,
        )

    barrier = pltpu.get_barrier_semaphore()
    peers = [sibling, across, diag_dev(1), diag_dev(-1)]
    peers += [z_dev(d) for d in range(1, 8)] + [chip_dev(jnp.int32(d)) for d in range(1, 8)]
    for dev in peers:
        pl.semaphore_signal(barrier, inc=1, device_id=dev, device_id_type=pl.DeviceIdType.MESH)

    pairs = [
        (acts_hbm, acts_ref), (tans_hbm, tans_ref), (v_hbm, v_ref), (w_hbm, w_ref), (rmask_hbm, rmask),
        (slope_hbm, slope_ref), (curv_hbm, curv_ref), (lmask_hbm, lmask),
    ]
    loads = [pltpu.make_async_copy(src, dst, l_s.at[n]) for n, (src, dst) in enumerate(pairs)]
    for c in loads:
        c.start()
    for c in loads[:2]:
        c.wait()

    both = jnp.concatenate([acts_ref[...].astype(F32), tans_ref[...].astype(F32)], axis=0)
    both = jnp.concatenate([both, jnp.zeros((16, LANES - PIXELS), F32)], axis=1)
    gath[filt] = both.astype(BF)
    pl.semaphore_wait(barrier, len(peers))

    mine = half * 8
    theirs = (1 - half) * 8
    right, left = z_dev(1), z_dev(-1)
    LOW, HIGH = pl.ds(0, CUT), pl.ds(CUT, LANES - CUT)

    def piece(slot, lanes, sem, dev):
        ref = gath.at[slot, :, lanes]
        return remote(ref, ref, send_s.at[0], sem, dev)

    def send(slot, lanes, *devs, cross=False):
        for dev in devs:
            if cross:
                sem = far_rs.at[0]
            else:
                sem = lo_rs.at[slot] if lanes is LOW else hi_rs.at[lax.rem(slot, 8)]
            piece(slot, lanes, sem, dev).start()

    def got(slot, lanes):
        sem = lo_rs.at[slot] if lanes is LOW else hi_rs.at[lax.rem(slot, 8)]
        piece(slot, lanes, sem, across).wait_recv()

    send(filt, LOW, diag_dev(1), diag_dev(-1))
    send(filt, HIGH, right, left)
    send(filt, LOW, right, left, across)
    send(filt, HIGH, across, cross=True)

    for c in loads[2:]:
        c.wait()
    for k in range(TAPS):
        vk = v_ref[k].astype(F32).reshape(16, 1, 8, 128)
        wk = w_ref[k].astype(F32).reshape(16, 1, 8, 128)
        wcat[:, 128 * k:128 * k + 128] = (
            jnp.concatenate([vk, wk], axis=1).reshape(256, 128).astype(BF)
        )
        taps[k, 0:PAD, :] = jnp.zeros((PAD, 128), F32)

    for h in range(1, 5):
        slot = mine + at_z(-h)
        got(slot, HIGH)
        if h < 4:
            send(slot, HIGH, right)
            if h == 3:
                send(slot, HIGH, diag_dev(1), cross=True)
            send(slot, HIGH, across, cross=True)
            slot = mine + at_z(h)
            got(slot, HIGH)
            if h < 3:
                send(slot, HIGH, left)
            send(slot, HIGH, across, cross=True)
        for group in (mine, theirs):
            slot = group + at_z(h)
            got(slot, LOW)
            if h < 4:
                send(slot, LOW, left)
                slot = group + at_z(-h)
                got(slot, LOW)
                if h < 3:
                    send(slot, LOW, right)

    got(theirs + z, LOW)

    def forward(t, _):
        lanes = pl.ds(pl.multiple_of(t * BLOCK, 128), BLOCK)
        rows = pl.ds(pl.multiple_of(PAD + t * BLOCK, 16), BLOCK)
        x = gath[:, :, lanes].reshape(256, BLOCK).T
        for k in range(0, TAPS, 2):
            width = min(2, TAPS - k)
            res = jnp.dot(x, wcat[:, 128 * k:128 * (k + width)], preferred_element_type=F32)
            for q in range(width):
                taps[k + q, rows, :] = res[:, 128 * q:128 * q + 128]
        return 0

    lax.fori_loop(0, CUT // BLOCK, forward, 0, unroll=True)
    cross = gath.at[pl.ds(theirs, 8), :, HIGH]
    remote(cross, cross, send_s.at[0], far_rs.at[0], across).wait_recv()
    lax.fori_loop(CUT // BLOCK, LANES // BLOCK, forward, 0, unroll=True)

    def combined(c, flip, part, put):
        start = c * SHARE
        within = lax.rem(start, IMAGE)
        first, count = PARTS[part]
        step = count // 2
        for s in range(first, first + count, step):
            m = [rmask[n, pl.ds(within + s, step), :] for n in range(4)]
            acc = None
            for a in range(3):
                row = None
                for e in range(3):
                    k = 3 * a + e
                    off = WW * (a - 1) + e - 1
                    val = taps[8 - k if flip else k, pl.ds(PAD + start + s + off, step), :]
                    if e == 0:
                        val = val * m[2]
                    if e == 2:
                        val = val * m[3]
                    row = val if row is None else row + val
                if a == 0:
                    row = row * m[0]
                if a == 2:
                    row = row * m[1]
                acc = row if acc is None else acc + row
            put(s, step, acc)

    def rows_of(part):
        return pl.ds(*PARTS[part])

    def sib_copy(d, part):
        return remote(
            sib_out.at[d, rows_of(part)], sib_in.at[d, rows_of(part)],
            send_s.at[1], s_rs.at[2 * d + part], sibling,
        )

    def to_sibling(i, part):
        d = chip_at(chip_turn(i))

        def put(s, n, acc):
            sib_out[d, s:s + n, :] = acc

        combined(2 * d + other, False, part, put)
        sib_copy(d, part).start()

    def red_copy(j, part):
        return remote(
            red_out.at[j, rows_of(part)], red_in.at[j, rows_of(part)],
            send_s.at[2], b_rs.at[part], chip_dev(j),
        )

    def to_chip(i, part):
        j = chip_turn(i)
        d = chip_at(j)
        sib_copy(d, part).wait_recv()

        def put(s, n, acc):
            red_out[j, s:s + n, :] = (acc + sib_in[d, s:s + n, :]).astype(BF)

        combined(2 * d + core, False, part, put)
        red_copy(j, part).start()

    def ahead(first, last, part, step=None, chip_part=None):
        def go(i, _):
            to_sibling(i, part)
            if step is not None:
                to_chip(i + step, chip_part)
            return 0

        lax.fori_loop(first, last, go, 0)

    def behind(i, _):
        to_chip(i, 1)
        return 0

    ahead(0, 4, 0)
    ahead(4, 8, 0, -4, 0)
    ahead(0, 3, 1, 4, 0)
    ahead(3, 4, 1)
    ahead(4, 8, 1, -4, 1)
    lax.fori_loop(4, 7, behind, 0)

    def put_own(s, n, acc):
        own[s:s + n, :] = acc + sib_in[chip, s:s + n, :]

    for part in range(2):
        sib_copy(chip, part).wait_recv()
        combined(2 * chip + core, False, part, put_own)

    def shift(t, _):
        g = gath[pl.ds(2 * t, 2)].astype(F32)
        x = g[:, 0:8, :].reshape(16, LANES)
        rows = pl.ds(pl.multiple_of(16 * t, 16), 16)
        for e in range(3):
            xe = x if e == 1 else pltpu.roll(x, (1 - e) % LANES, 1)
            for a in range(3):
                k = 3 * a + e
                xk = xe if a == 1 else pltpu.roll(xe, (WW * (1 - a)) % LANES, 1)
                xts[k, rows, :] = (xk * lmask[k:k + 1, :]).astype(BF)
        return 0

    lax.fori_loop(0, 4, shift, 0)

    def wgt_copy(slot, part, dev):
        ref = wgt.at[slot, rows_of(part)]
        return remote(ref, ref, send_s.at[3], w_rs.at[2 * lax.div(slot, 2) + part], dev)

    def sib_wgt_copy(slot, part):
        ref = wgt.at[slot, rows_of(part)]
        return remote(ref, ref, send_s.at[3], p_rs.at[part], sibling)

    for part, (first, count) in enumerate(PARTS):
        rows = slice(first, first + count)

        all_in = red_in.at[pl.ds(1, 7), rows_of(part)]
        remote(all_in, all_in, send_s.at[2], b_rs.at[part], sibling).wait_recv()
        total = own[rows, :]
        for j in range(1, 8):
            total = total + red_in[j, rows, :].astype(F32)
        valid = min(first + count, SHARE) - first
        slope = slope_ref[first:first + valid, :].astype(F32)
        curv = curv_ref[first:first + valid, :].astype(F32)
        weighted = slope * slope * curv * total[:valid]
        if valid < count:
            weighted = jnp.concatenate([weighted, jnp.zeros((count - valid, 128), F32)], axis=0)
        wgt[chan, rows, :] = weighted.astype(BF)

        def spread(i, _, part=part):
            j = chip_turn(i)
            wgt_copy(chan, part, chip_dev(j)).start()
            return 0

        lax.fori_loop(0, 7, spread, 0)
        sib_wgt_copy(chan, part).start()

    lax.fori_loop(4, 8, shift, 0)

    def unpack(c, part):
        start = c * SHARE
        first, count = PARTS[part]
        x = wgt[c, rows_of(part), :].astype(F32)
        if part == 0:
            w32[pl.ds(start, count), :] = x
        else:
            w32[pl.ds(start + first, 160 - first), :] = x[0:160 - first]
            w32[pl.ds(start + 160, 2), :] = x[160 - first:162 - first]

    for part in range(2):

        def pass_on(i, _, part=part):
            j = chip_turn(i)
            slot = 2 * chip_at(j, -1) + core
            wgt_copy(slot, part, sibling).wait_recv()
            sib_wgt_copy(slot, part).start()
            unpack(slot, part)
            return 0

        unpack(chan, part)
        lax.fori_loop(0, 7, pass_on, 0)

    for part in range(2):

        def from_sibling(i, _, part=part):
            unpack(2 * i + other, part)
            return 0

        passed = wgt.at[pl.ds(0, 8), rows_of(part)]
        remote(passed, passed, send_s.at[3], p_rs.at[part], sibling).wait_recv()

        lax.fori_loop(0, 8, from_sibling, 0)
    w32[PIXELS:LANES, :] = jnp.zeros((LANES - PIXELS, 128), F32)

    def backward(i, _, early=False):
        base = 3 * (1 - half)
        if early:
            start = (theirs + at_z(4)) * SHARE - WW - 1
            block = lax.div(lax.max(start, 0), BLOCK)
            t = base + lax.rem(block - base + i, 4)
        else:
            t = lax.rem(i + base, LANES // BLOCK)
        rows = pl.ds(pl.multiple_of(t * BLOCK, 16), BLOCK)
        spot = pl.ds(pl.multiple_of(PAD + t * BLOCK, 16), BLOCK)
        w = w32[rows, :].astype(BF)
        w16[rows, :] = w
        for k in range(0, TAPS, 2):
            width = min(2, TAPS - k)
            kern = w_ref[k:k + width].reshape(128 * width, 128)
            res = lax.dot_general(w, kern, (((1,), (1,)), ((), ())), preferred_element_type=F32)
            for q in range(width):
                taps[k + q, spot, :] = res[:, 128 * q:128 * q + 128]
        return 0

    def early(i, _):
        return backward(i, 0, True)

    lax.fori_loop(0, 2, early, 0, unroll=True)

    scale = F32(1.0) / jnp.sqrt(F32(PIXELS))

    def kp_copy(k):
        return pltpu.make_async_copy(kp_ref.at[k], kp_hbm.at[k], k_s.at[0])

    def product(k):
        kp_ref[k] = jnp.dot(xts[k], w16[...], preferred_element_type=F32) * scale
        kp_copy(k).start()

    def cx_copy(j, part):
        return remote(
            cx_out.at[j, rows_of(part)], cx_in.at[j, rows_of(part)],
            send_s.at[4], x_rs.at[2 * j + part], across,
        )

    def cz_copy(j, part):
        return remote(
            cz_out.at[j, rows_of(part)], cz_in.at[j, rows_of(part)],
            send_s.at[5], d_rs.at[0], z_dev(j),
        )

    def to_across(i, _):
        j = z_turn(i)

        def put(s, n, acc):
            cx_out[j, s:s + n, :] = acc.astype(BF)

        for part in range(2):
            combined(theirs + at_z(j), True, part, put)
            cx_copy(j, part).start()
        return 0

    to_across(0, 0)
    lax.fori_loop(2, 4, early, 0, unroll=True)
    lax.fori_loop(1, 8, to_across, 0)
    lax.fori_loop(4, LANES // BLOCK, backward, 0, unroll=True)

    def to_z(i, _):
        j = z_turn(i)

        def put(s, n, acc):
            cz_out[j, s:s + n, :] = (acc + cx_in[j, s:s + n, :].astype(F32)).astype(BF)

        for part in range(2):
            cx_copy(j, part).wait_recv()
            combined(mine + at_z(j), True, part, put)
            cz_copy(j, part).start()
        product(i)
        return 0

    lax.fori_loop(0, 7, to_z, 0)

    def put_last(s, n, acc):
        own[s:s + n, :] = acc + cx_in[0, s:s + n, :].astype(F32)

    for part in range(2):
        cx_copy(0, part).wait_recv()
        combined(mine + z, True, part, put_last)
    product(7)
    product(8)

    others = pl.ds(1, 7)
    remote(cz_in.at[others], cz_in.at[others], send_s.at[5], d_rs.at[0], across).wait_recv()
    total = own[...]
    for j in range(1, 8):
        total = total + cz_in[j].astype(F32)
    cot_ref[...] = total[0:SHARE].astype(BF)

    pltpu.make_async_copy(kp_ref, kp_hbm, k_s.at[0]).wait()
    spent = [
        gath.at[pl.ds(0, 15)], sib_out, red_out.at[others],
        wgt.at[pl.ds(0, 15)], cx_out, cz_out.at[others],
    ]
    for n, ref in enumerate(spent):
        remote(ref, ref, send_s.at[n], d_rs.at[0], across).wait_send()


def settle(cot_in, kp_in, cot_ref, kp_ref, cot_v, kp_v, in_s, out_s):
    legs = [(cot_in, cot_v, cot_ref)]
    for n in range(3):
        part = pl.ds(3 * n, 3)
        legs.append((kp_in.at[part], kp_v.at[part], kp_ref.at[part]))
    for n, (src, via, _) in enumerate(legs):
        pltpu.make_async_copy(src, via, in_s.at[n]).start()
    for n, (src, via, dst) in enumerate(legs):
        pltpu.make_async_copy(src, via, in_s.at[n]).wait()
        pltpu.make_async_copy(via, dst, out_s.at[n]).start()
    for n, (_, via, dst) in enumerate(legs):
        pltpu.make_async_copy(via, dst, out_s.at[n]).wait()


def per_device(activations, act_tangent, kernel, kernel_tangent, slope, curvature):
    vm = pl.BlockSpec(memory_space=pltpu.VMEM)
    hbm = pl.BlockSpec(memory_space=pl.ANY)
    dma = pltpu.SemaphoreType.DMA
    share = (8, ROWS, 128)
    shapes = (
        jax.ShapeDtypeStruct((SHARE, 128), BF),
        jax.ShapeDtypeStruct((TAPS, 128, 128), F32),
    )
    results = pl.pallas_call(
        body,
        out_shape=shapes,
        in_specs=[hbm] * 8,
        out_specs=(vm, hbm),
        scratch_shapes=[
            pltpu.VMEM((8, PIXELS), BF),
            pltpu.VMEM((8, PIXELS), BF),
            pltpu.VMEM((TAPS, 128, 128), BF),
            pltpu.VMEM((TAPS, 128, 128), BF),
            pltpu.VMEM((SHARE, 128), BF),
            pltpu.VMEM((SHARE, 128), BF),
            pltpu.VMEM((4, IMAGE + ROWS, 128), F32),
            pltpu.VMEM((16, LANES), F32),
            pltpu.VMEM((TAPS, 128, 128), F32),
            pltpu.VMEM((16, 16, LANES), BF),
            pltpu.VMEM((256, TAPS * 128), BF),
            pltpu.VMEM((TAPS, PAD + LANES, 128), F32),
            pltpu.VMEM((TAPS, 128, LANES), BF),
            pltpu.VMEM((PAD + LANES, 128), F32),
            pltpu.VMEM((LANES, 128), BF),
            pltpu.VMEM(share, F32),
            pltpu.VMEM(share, F32),
            pltpu.VMEM(share, BF),
            pltpu.VMEM(share, BF),
            pltpu.VMEM((ROWS, 128), F32),
            pltpu.VMEM((16, ROWS, 128), BF),
            pltpu.VMEM(share, BF),
            pltpu.VMEM(share, BF),
            pltpu.VMEM(share, BF),
            pltpu.VMEM(share, BF),
            dma((8,)), dma((1,)), dma((6,)),
            dma((16,)), dma((8,)), dma((1,)), dma((16,)), dma((2,)),
            dma((16,)), dma((2,)), dma((16,)), dma((1,)),
        ],
        compiler_params=pltpu.CompilerParams(
            collective_id=0, has_side_effects=True, vmem_limit_bytes=56 * 1024 * 1024
        ),
        name="gauss_newton",
    )(
        activations.T, act_tangent.T, kernel, kernel_tangent, slope, curvature,
        jnp.asarray(row_masks()), jnp.asarray(lane_masks()),
    )
    return pl.pallas_call(
        settle,
        out_shape=shapes,
        in_specs=[hbm, hbm],
        out_specs=(hbm, hbm),
        scratch_shapes=[
            pltpu.VMEM((SHARE, 128), BF), pltpu.VMEM((TAPS, 128, 128), F32), dma((4,)), dma((4,))
        ],
        name="settle",
    )(*results)


def solution(mesh):
    return jax.shard_map(
        per_device,
        mesh=mesh,
        in_specs=(
            P(None, ("chan", "filt")),
            P(None, ("chan", "filt")),
            P(None, "chan", "filt"),
            P(None, "chan", "filt"),
            P("chan", "filt"),
            P("chan", "filt"),
        ),
        out_specs=(P("filt", "chan"), P(None, "chan", "filt")),
        check_vma=False,
    )
```

```python
import jax
import jax.numpy as jnp
import numpy as np
from jax import lax
from jax.experimental import pallas as pl
from jax.experimental.pallas import tpu as pltpu
from jax.sharding import PartitionSpec as P

HH = 12
WW = 12
IMAGE = HH * WW
PIXELS = 2592
LANES = 2688
CUT = 1152
SHARE = 162
ROWS = 176
PARTS = ((0, 80), (80, 96))
PAD = 16
BLOCK = 384
TAPS = 9
BF = jnp.bfloat16
F32 = jnp.float32


def row_masks():
    r = np.arange(IMAGE + ROWS)
    i, j = (r // WW) % HH, r % WW
    m = np.stack([i >= 1, i <= HH - 2, j >= 1, j <= WW - 2]).astype(np.float32)
    return np.ascontiguousarray(np.broadcast_to(m[:, :, None], (*m.shape, 128)))


def lane_masks():
    p = np.arange(LANES)
    i, j = (p // WW) % HH, p % WW
    m = np.zeros((16, LANES), np.float32)
    for a in range(3):
        for e in range(3):
            si, sj = i + a - 1, j + e - 1
            m[3 * a + e] = (si >= 0) & (si < HH) & (sj >= 0) & (sj < WW) & (p < PIXELS)
    return m


def body(
    acts_hbm, tans_hbm, w_hbm, v_hbm, slope_hbm, curv_hbm, rmask_hbm, lmask_hbm,
    cot_ref, kp_hbm,
    acts_ref, tans_ref, w_ref, v_ref, slope_ref, curv_ref, rmask, lmask, kp_ref,
    gath, wcat, taps, xts, w32, w16, sib_out, sib_in, red_out, red_in, own,
    wgt, cx_out, cx_in, cz_out, cz_in,
    l_s, k_s,
    send_s, lo_rs, hi_rs, far_rs, s_rs, b_rs, w_rs, p_rs, x_rs, d_rs,
):
    chan = lax.axis_index("chan")
    filt = lax.axis_index("filt")
    core = lax.rem(chan, 2)
    chip = lax.div(chan, 2)
    half = lax.div(filt, 8)
    z = lax.rem(filt, 8)
    other = 1 - core
    sibling = {"chan": 2 * chip + other, "filt": filt}
    across = {"chan": chan, "filt": (1 - half) * 8 + z}

    def at_z(d):
        return lax.rem(z + d + 8, 8)

    def z_dev(d):
        return {"chan": chan, "filt": half * 8 + at_z(d)}

    def diag_dev(d):
        return {"chan": chan, "filt": (1 - half) * 8 + at_z(d)}

    def chip_at(j, sign=1):
        row = lax.rem(lax.div(chip, 2) + sign * lax.div(j, 2) + 4, 4)
        return 2 * row + lax.rem(chip + j, 2)

    def chip_dev(j):
        return {"chan": 2 * chip_at(j) + core, "filt": filt}

    def turns(i, middle):
        return middle + (1 - 2 * lax.rem(i, 2)) * lax.div(i + 1, 2)

    def chip_turn(i):
        return 2 * turns(lax.rem(i, 4), 2) + 1 - lax.div(i, 4)

    def z_turn(i):
        return turns(i, 4)

    def remote(src, dst, ss, rs, dev):
        return pltpu.make_async_remote_copy(
            src_ref=src, dst_ref=dst, send_sem=ss, recv_sem=rs,
            device_id=dev, device_id_type=pl.DeviceIdType.MESH,
        )

    barrier = pltpu.get_barrier_semaphore()
    peers = [sibling, across, diag_dev(1), diag_dev(-1)]
    peers += [z_dev(1), z_dev(-1)] + [chip_dev(jnp.int32(d)) for d in range(1, 8)]
    for dev in peers:
        pl.semaphore_signal(barrier, inc=1, device_id=dev, device_id_type=pl.DeviceIdType.MESH)

    pairs = [
        (acts_hbm, acts_ref), (tans_hbm, tans_ref), (v_hbm, v_ref), (w_hbm, w_ref), (rmask_hbm, rmask),
        (slope_hbm, slope_ref), (curv_hbm, curv_ref), (lmask_hbm, lmask),
    ]
    loads = [pltpu.make_async_copy(src, dst, l_s.at[n]) for n, (src, dst) in enumerate(pairs)]
    for c in loads:
        c.start()
    for c in loads[:2]:
        c.wait()

    both = jnp.concatenate([acts_ref[...].astype(F32), tans_ref[...].astype(F32)], axis=0)
    both = jnp.concatenate([both, jnp.zeros((16, LANES - PIXELS), F32)], axis=1)
    gath[filt] = both.astype(BF)
    pl.semaphore_wait(barrier, len(peers))

    mine = half * 8
    theirs = (1 - half) * 8
    right, left = z_dev(1), z_dev(-1)
    LOW, HIGH = pl.ds(0, CUT), pl.ds(CUT, LANES - CUT)

    def piece(slot, lanes, sem, dev):
        ref = gath.at[slot, :, lanes]
        return remote(ref, ref, send_s.at[0], sem, dev)

    def send(slot, lanes, *devs, cross=False):
        for dev in devs:
            if cross:
                sem = far_rs.at[0]
            else:
                sem = lo_rs.at[slot] if lanes is LOW else hi_rs.at[lax.rem(slot, 8)]
            piece(slot, lanes, sem, dev).start()

    def got(slot, lanes):
        sem = lo_rs.at[slot] if lanes is LOW else hi_rs.at[lax.rem(slot, 8)]
        piece(slot, lanes, sem, across).wait_recv()

    send(filt, LOW, diag_dev(1), diag_dev(-1))
    send(filt, HIGH, right, left)
    send(filt, LOW, right, left, across)
    send(filt, HIGH, across, cross=True)

    for c in loads[2:]:
        c.wait()
    for k in range(TAPS):
        vk = v_ref[k].astype(F32).reshape(16, 1, 8, 128)
        wk = w_ref[k].astype(F32).reshape(16, 1, 8, 128)
        wcat[:, 128 * k:128 * k + 128] = (
            jnp.concatenate([vk, wk], axis=1).reshape(256, 128).astype(BF)
        )
        taps[k, 0:PAD, :] = jnp.zeros((PAD, 128), F32)

    for h in range(1, 5):
        slot = mine + at_z(-h)
        got(slot, HIGH)
        if h < 4:
            send(slot, HIGH, right)
            if h == 3:
                send(slot, HIGH, diag_dev(1), cross=True)
            send(slot, HIGH, across, cross=True)
            slot = mine + at_z(h)
            got(slot, HIGH)
            if h < 3:
                send(slot, HIGH, left)
            send(slot, HIGH, across, cross=True)
        for group in (mine, theirs):
            slot = group + at_z(h)
            got(slot, LOW)
            if h < 4:
                send(slot, LOW, left)
                slot = group + at_z(-h)
                got(slot, LOW)
                if h < 3:
                    send(slot, LOW, right)

    got(theirs + z, LOW)

    def forward(t, _):
        lanes = pl.ds(pl.multiple_of(t * BLOCK, 128), BLOCK)
        rows = pl.ds(pl.multiple_of(PAD + t * BLOCK, 16), BLOCK)
        x = gath[:, :, lanes].reshape(256, BLOCK).T
        for k in range(0, TAPS, 2):
            width = min(2, TAPS - k)
            res = jnp.dot(x, wcat[:, 128 * k:128 * (k + width)], preferred_element_type=F32)
            for q in range(width):
                taps[k + q, rows, :] = res[:, 128 * q:128 * q + 128]
        return 0

    lax.fori_loop(0, CUT // BLOCK, forward, 0, unroll=True)
    cross = gath.at[pl.ds(theirs, 8), :, HIGH]
    remote(cross, cross, send_s.at[0], far_rs.at[0], across).wait_recv()
    lax.fori_loop(CUT // BLOCK, LANES // BLOCK, forward, 0, unroll=True)

    def combined(c, flip, part, put):
        start = c * SHARE
        within = lax.rem(start, IMAGE)
        first, count = PARTS[part]
        step = count // 2
        for s in range(first, first + count, step):
            m = [rmask[n, pl.ds(within + s, step), :] for n in range(4)]
            acc = None
            for a in range(3):
                row = None
                for e in range(3):
                    k = 3 * a + e
                    off = WW * (a - 1) + e - 1
                    val = taps[8 - k if flip else k, pl.ds(PAD + start + s + off, step), :]
                    if e == 0:
                        val = val * m[2]
                    if e == 2:
                        val = val * m[3]
                    row = val if row is None else row + val
                if a == 0:
                    row = row * m[0]
                if a == 2:
                    row = row * m[1]
                acc = row if acc is None else acc + row
            put(s, step, acc)

    def rows_of(part):
        return pl.ds(*PARTS[part])

    def sib_copy(d, part):
        return remote(
            sib_out.at[d, rows_of(part)], sib_in.at[d, rows_of(part)],
            send_s.at[1], s_rs.at[2 * d + part], sibling,
        )

    def to_sibling(i, part):
        d = chip_at(chip_turn(i))

        def put(s, n, acc):
            sib_out[d, s:s + n, :] = acc

        combined(2 * d + other, False, part, put)
        sib_copy(d, part).start()

    def red_copy(j, part):
        return remote(
            red_out.at[j, rows_of(part)], red_in.at[j, rows_of(part)],
            send_s.at[2], b_rs.at[part], chip_dev(j),
        )

    def to_chip(i, part):
        j = chip_turn(i)
        d = chip_at(j)
        sib_copy(d, part).wait_recv()

        def put(s, n, acc):
            red_out[j, s:s + n, :] = (acc + sib_in[d, s:s + n, :]).astype(BF)

        combined(2 * d + core, False, part, put)
        red_copy(j, part).start()

    def ahead(first, last, part, step=None, chip_part=None):
        def go(i, _):
            to_sibling(i, part)
            if step is not None:
                to_chip(i + step, chip_part)
            return 0

        lax.fori_loop(first, last, go, 0)

    def behind(i, _):
        to_chip(i, 1)
        return 0

    ahead(0, 4, 0)
    ahead(4, 8, 0, -4, 0)
    ahead(0, 3, 1, 4, 0)
    ahead(3, 4, 1)
    ahead(4, 8, 1, -4, 1)
    lax.fori_loop(4, 7, behind, 0)

    def put_own(s, n, acc):
        own[s:s + n, :] = acc + sib_in[chip, s:s + n, :]

    for part in range(2):
        sib_copy(chip, part).wait_recv()
        combined(2 * chip + core, False, part, put_own)

    def shift(t, _):
        g = gath[pl.ds(2 * t, 2)].astype(F32)
        x = g[:, 0:8, :].reshape(16, LANES)
        rows = pl.ds(pl.multiple_of(16 * t, 16), 16)
        for e in range(3):
            xe = x if e == 1 else pltpu.roll(x, (1 - e) % LANES, 1)
            for a in range(3):
                k = 3 * a + e
                xk = xe if a == 1 else pltpu.roll(xe, (WW * (1 - a)) % LANES, 1)
                xts[k, rows, :] = (xk * lmask[k:k + 1, :]).astype(BF)
        return 0

    lax.fori_loop(0, 4, shift, 0)

    def wgt_copy(slot, part, dev):
        ref = wgt.at[slot, rows_of(part)]
        return remote(ref, ref, send_s.at[3], w_rs.at[2 * lax.div(slot, 2) + part], dev)

    def sib_wgt_copy(slot, part):
        ref = wgt.at[slot, rows_of(part)]
        return remote(ref, ref, send_s.at[3], p_rs.at[part], sibling)

    for part, (first, count) in enumerate(PARTS):
        rows = slice(first, first + count)

        all_in = red_in.at[pl.ds(1, 7), rows_of(part)]
        remote(all_in, all_in, send_s.at[2], b_rs.at[part], sibling).wait_recv()
        total = own[rows, :]
        for j in range(1, 8):
            total = total + red_in[j, rows, :].astype(F32)
        valid = min(first + count, SHARE) - first
        slope = slope_ref[first:first + valid, :].astype(F32)
        curv = curv_ref[first:first + valid, :].astype(F32)
        weighted = slope * slope * curv * total[:valid]
        if valid < count:
            weighted = jnp.concatenate([weighted, jnp.zeros((count - valid, 128), F32)], axis=0)
        wgt[chan, rows, :] = weighted.astype(BF)

        def spread(i, _, part=part):
            j = chip_turn(i)
            wgt_copy(chan, part, chip_dev(j)).start()
            return 0

        lax.fori_loop(0, 7, spread, 0)
        sib_wgt_copy(chan, part).start()

    lax.fori_loop(4, 8, shift, 0)

    def unpack(c, part):
        start = c * SHARE
        first, count = PARTS[part]
        x = wgt[c, rows_of(part), :].astype(F32)
        if part == 0:
            w32[pl.ds(start, count), :] = x
        else:
            w32[pl.ds(start + first, 160 - first), :] = x[0:160 - first]
            w32[pl.ds(start + 160, 2), :] = x[160 - first:162 - first]

    for part in range(2):

        def pass_on(i, _, part=part):
            j = chip_turn(i)
            slot = 2 * chip_at(j, -1) + core
            wgt_copy(slot, part, sibling).wait_recv()
            sib_wgt_copy(slot, part).start()
            unpack(slot, part)
            return 0

        unpack(chan, part)
        lax.fori_loop(0, 7, pass_on, 0)

    for part in range(2):

        def from_sibling(i, _, part=part):
            unpack(2 * i + other, part)
            return 0

        passed = wgt.at[pl.ds(0, 8), rows_of(part)]
        remote(passed, passed, send_s.at[3], p_rs.at[part], sibling).wait_recv()

        lax.fori_loop(0, 8, from_sibling, 0)
    w32[PIXELS:LANES, :] = jnp.zeros((LANES - PIXELS, 128), F32)

    def backward(i, _, early=False):
        base = 3 * (1 - half)
        if early:
            start = (theirs + at_z(4)) * SHARE - WW - 1
            block = lax.div(lax.max(start, 0), BLOCK)
            t = base + lax.rem(block - base + i, 4)
        else:
            t = lax.rem(i + base, LANES // BLOCK)
        rows = pl.ds(pl.multiple_of(t * BLOCK, 16), BLOCK)
        spot = pl.ds(pl.multiple_of(PAD + t * BLOCK, 16), BLOCK)
        w = w32[rows, :].astype(BF)
        w16[rows, :] = w
        for k in range(0, TAPS, 2):
            width = min(2, TAPS - k)
            kern = w_ref[k:k + width].reshape(128 * width, 128)
            res = lax.dot_general(w, kern, (((1,), (1,)), ((), ())), preferred_element_type=F32)
            for q in range(width):
                taps[k + q, spot, :] = res[:, 128 * q:128 * q + 128]
        return 0

    def early(i, _):
        return backward(i, 0, True)

    lax.fori_loop(0, 2, early, 0, unroll=True)

    scale = F32(1.0) / jnp.sqrt(F32(PIXELS))

    def kp_copy(k):
        return pltpu.make_async_copy(kp_ref.at[k], kp_hbm.at[k], k_s.at[0])

    def product(k):
        kp_ref[k] = jnp.dot(xts[k], w16[...], preferred_element_type=F32) * scale
        kp_copy(k).start()

    def cx_copy(j, part):
        return remote(
            cx_out.at[j, rows_of(part)], cx_in.at[j, rows_of(part)],
            send_s.at[4], x_rs.at[2 * j + part], across,
        )

    def cz_copy(j, part):
        return remote(
            cz_out.at[j, rows_of(part)], cz_in.at[j, rows_of(part)],
            send_s.at[5], d_rs.at[0], z_dev(j),
        )

    def to_across(i, _):
        j = z_turn(i)

        def put(s, n, acc):
            cx_out[j, s:s + n, :] = acc.astype(BF)

        for part in range(2):
            combined(theirs + at_z(j), True, part, put)
            cx_copy(j, part).start()
        return 0

    to_across(0, 0)
    lax.fori_loop(2, 4, early, 0, unroll=True)
    lax.fori_loop(1, 8, to_across, 0)
    lax.fori_loop(4, LANES // BLOCK, backward, 0, unroll=True)

    def to_z(i, _):
        j = z_turn(i)

        def put(s, n, acc):
            cz_out[j, s:s + n, :] = (acc + cx_in[j, s:s + n, :].astype(F32)).astype(BF)

        for part in range(2):
            cx_copy(j, part).wait_recv()
            combined(mine + at_z(j), True, part, put)
            cz_copy(j, part).start()
        product(i)
        return 0

    lax.fori_loop(0, 7, to_z, 0)

    def put_last(s, n, acc):
        own[s:s + n, :] = acc + cx_in[0, s:s + n, :].astype(F32)

    for part in range(2):
        cx_copy(0, part).wait_recv()
        combined(mine + z, True, part, put_last)
    product(7)
    product(8)

    others = pl.ds(1, 7)
    remote(cz_in.at[others], cz_in.at[others], send_s.at[5], d_rs.at[0], across).wait_recv()
    total = own[...]
    for j in range(1, 8):
        total = total + cz_in[j].astype(F32)
    cot_ref[...] = total[0:SHARE].astype(BF)

    pltpu.make_async_copy(kp_ref, kp_hbm, k_s.at[0]).wait()
    spent = [
        gath.at[pl.ds(0, 15)], sib_out, red_out.at[others],
        wgt.at[pl.ds(0, 15)], cx_out, cz_out.at[others],
    ]
    for n, ref in enumerate(spent):
        remote(ref, ref, send_s.at[n], d_rs.at[0], across).wait_send()


def settle(cot_in, kp_in, cot_ref, kp_ref, cot_v, kp_v, in_s, out_s):
    legs = [(cot_in, cot_v, cot_ref)]
    for n in range(3):
        part = pl.ds(3 * n, 3)
        legs.append((kp_in.at[part], kp_v.at[part], kp_ref.at[part]))
    for n, (src, via, _) in enumerate(legs):
        pltpu.make_async_copy(src, via, in_s.at[n]).start()
    for n, (src, via, dst) in enumerate(legs):
        pltpu.make_async_copy(src, via, in_s.at[n]).wait()
        pltpu.make_async_copy(via, dst, out_s.at[n]).start()
    for n, (_, via, dst) in enumerate(legs):
        pltpu.make_async_copy(via, dst, out_s.at[n]).wait()


def per_device(activations, act_tangent, kernel, kernel_tangent, slope, curvature):
    vm = pl.BlockSpec(memory_space=pltpu.VMEM)
    hbm = pl.BlockSpec(memory_space=pl.ANY)
    dma = pltpu.SemaphoreType.DMA
    share = (8, ROWS, 128)
    shapes = (
        jax.ShapeDtypeStruct((SHARE, 128), BF),
        jax.ShapeDtypeStruct((TAPS, 128, 128), F32),
    )
    results = pl.pallas_call(
        body,
        out_shape=shapes,
        in_specs=[hbm] * 8,
        out_specs=(vm, hbm),
        scratch_shapes=[
            pltpu.VMEM((8, PIXELS), BF),
            pltpu.VMEM((8, PIXELS), BF),
            pltpu.VMEM((TAPS, 128, 128), BF),
            pltpu.VMEM((TAPS, 128, 128), BF),
            pltpu.VMEM((SHARE, 128), BF),
            pltpu.VMEM((SHARE, 128), BF),
            pltpu.VMEM((4, IMAGE + ROWS, 128), F32),
            pltpu.VMEM((16, LANES), F32),
            pltpu.VMEM((TAPS, 128, 128), F32),
            pltpu.VMEM((16, 16, LANES), BF),
            pltpu.VMEM((256, TAPS * 128), BF),
            pltpu.VMEM((TAPS, PAD + LANES, 128), F32),
            pltpu.VMEM((TAPS, 128, LANES), BF),
            pltpu.VMEM((PAD + LANES, 128), F32),
            pltpu.VMEM((LANES, 128), BF),
            pltpu.VMEM(share, F32),
            pltpu.VMEM(share, F32),
            pltpu.VMEM(share, BF),
            pltpu.VMEM(share, BF),
            pltpu.VMEM((ROWS, 128), F32),
            pltpu.VMEM((16, ROWS, 128), BF),
            pltpu.VMEM(share, BF),
            pltpu.VMEM(share, BF),
            pltpu.VMEM(share, BF),
            pltpu.VMEM(share, BF),
            dma((8,)), dma((1,)), dma((6,)),
            dma((16,)), dma((8,)), dma((1,)), dma((16,)), dma((2,)),
            dma((16,)), dma((2,)), dma((16,)), dma((1,)),
        ],
        compiler_params=pltpu.CompilerParams(
            collective_id=0, has_side_effects=True, vmem_limit_bytes=56 * 1024 * 1024
        ),
        name="gauss_newton",
    )(
        activations.T, act_tangent.T, kernel, kernel_tangent, slope, curvature,
        jnp.asarray(row_masks()), jnp.asarray(lane_masks()),
    )
    return pl.pallas_call(
        settle,
        out_shape=shapes,
        in_specs=[hbm, hbm],
        out_specs=(hbm, hbm),
        scratch_shapes=[
            pltpu.VMEM((SHARE, 128), BF), pltpu.VMEM((TAPS, 128, 128), F32), dma((4,)), dma((4,))
        ],
        name="settle",
    )(*results)


def solution(mesh):
    return jax.shard_map(
        per_device,
        mesh=mesh,
        in_specs=(
            P(None, ("chan", "filt")),
            P(None, ("chan", "filt")),
            P(None, "chan", "filt"),
            P(None, "chan", "filt"),
            P("chan", "filt"),
            P("chan", "filt"),
        ),
        out_specs=(P("filt", "chan"), P(None, "chan", "filt")),
        check_vma=False,
    )
```
